256 devices in a mesh: subj: 4 (over y), vert: 64 (over x, z, core).
Axes of the slice: x: 4, y: 4, z: 8, core: 2. Of those that a mesh axis runs over, the one named last changes fastest.
Arguments:
- series: bfloat16 [4096, 98304], P('subj', 'vert'), parts along dimension 0, may hold values from -6 to 6
- labels: int32 [98304], P('vert'), may hold values from 0 to 1023
- tier_index: int32 [12288], P('vert'), may hold values from 0 to 1535
- template: bfloat16 [12288, 1024], P('vert'), may hold values from -12 to 12
Outputs:
- profiles: bfloat16 [12288, 4096], P('vert', 'subj'), parts along dimension 1
- rotation: float32 [1024, 4096], P('vert', 'subj'), parts along dimension 1
The draws below stay inside these ranges and needn't reach their ends.
There are 4 independent parts, one for each index of `subj`. The reference program is written for one: setup_inputs(seed, part) draws one part's arguments, and reference() takes and returns one part's arrays. A program takes and returns all parts, laid end to end along the dimension named above; an argument that names none is the same for every part. Nothing has to cross between parts.
All inputs are finite; a program needn't handle non-finite values.
Results may differ from the reference program's by a relative error of at most 0.0015.
The reference program's roundings to bfloat16 on the way (of `parcel_z` and `vertex_z`) count: a program that leaves them out, or rounds other values in their place, can miss the bound.
Values may be sent and summed in bfloat16 or wider, within the bound.
A program may use at most 64 MiB of HBM per device.

```python
import math
import jax
import jax.numpy as jnp
import numpy as np
from jax import lax

FRAMES = 1024
GRAY_DEV = 1536
TIER_DEV = 192
NS_STEPS = 4
PARCELS = 1024
GRAY = 98304
TIER = 12288


def draw_template(key, part):
    key = jax.random.fold_in(key, 7)
    noise_key, row_key, col_key = jax.random.split(key, 3)
    noise = jax.random.truncated_normal(noise_key, -6.0, 6.0, (TIER, PARCELS), jnp.float32)
    row_part = 1.1 * jax.random.truncated_normal(row_key, -2.7, 2.7, (TIER,), jnp.float32)
    col_part = jnp.exp(jax.random.uniform(col_key, (PARCELS,), jnp.float32, math.log(0.4), math.log(2.0)))
    return (noise + row_part[:, None] * col_part[None, :]).astype(jnp.bfloat16)


def plant(result, rng, low, high):
    place = [jax.random.randint(jax.random.fold_in(rng, axis), (), 0, length) for axis, length in enumerate(result.shape)]
    main_axis = result.shape.index(max(result.shape))
    next_to = place[:main_axis] + [(place[main_axis] + 1) % result.shape[main_axis]] + place[main_axis + 1:]
    return result.at[tuple(place)].set(low).at[tuple(next_to)].set(high)


def level_of(key, shape, cuts, smallest, high):
    gain = 1.0
    for axis_at, parts in cuts:
        heights = jax.random.uniform(jax.random.fold_in(jax.random.fold_in(key, 6), axis_at), (parts,), jnp.float32, smallest / len(cuts), high / len(cuts))
        gain = gain * jnp.repeat(jnp.exp(heights), shape[axis_at] // parts).reshape((-1,) + (1,) * (len(shape) - 1 - axis_at))
    return gain


def cumulative_ranks(number_of, slope):
    portions = [(1 << 20) // math.isqrt(grade ** slope) + 1 for grade in range(1, number_of + 1)]
    scale = 1 + sum(portions) // (1 << 30)
    return np.cumsum(np.array([max(1, weight // scale) for weight in portions]))


def ranked(own_key, extent, amount, lean):
    table = cumulative_ranks(amount, lean)
    lot = jax.random.randint(jax.random.fold_in(own_key, 1), extent, 0, int(table[amount - 1]))
    rank = jnp.searchsorted(jnp.asarray(table, jnp.int32), lot, side="right")
    return jax.random.permutation(jax.random.fold_in(own_key, 2), amount)[rank].astype(jnp.int32)


def bell_draw(rng, extent, deviation, bound, cuts=(), held_as=jnp.bfloat16):
    values = deviation * jax.random.normal(rng, extent, jnp.float32)
    if cuts:
        values = values * level_of(rng, extent, cuts, -0.22, 0.18)
    return jnp.clip(values, -bound, bound).astype(held_as)


def setup_inputs(seed: int = 0, part: int = 0) -> dict:
    streams_of = jax.random.split(jax.random.key(seed), 5)
    part_keys = jax.random.split(jax.random.fold_in(streams_of[4], part), 5)
    series = bell_draw(part_keys[0], (FRAMES, GRAY), 1.0, 6.0, ((1, 64),))
    labels = plant(ranked(streams_of[1], (GRAY,), PARCELS, 1), jax.random.fold_in(streams_of[1], 3), 0, PARCELS - 1).astype(jnp.int32)
    tier_index = plant(jax.random.randint(streams_of[2], (TIER,), 0, GRAY_DEV), jax.random.fold_in(streams_of[2], 1), 0, GRAY_DEV - 1).astype(jnp.int32)
    template = draw_template(jax.random.fold_in(streams_of[4], 71), part)
    return dict(series=series, labels=labels, tier_index=tier_index, template=template)


def standardize(block):
    centered = block - lax.optimization_barrier(jnp.mean(block, axis=0, keepdims=True))
    return centered / jnp.sqrt(lax.optimization_barrier(jnp.mean(centered * centered, axis=0, keepdims=True)) + 1e-05)

def reference(series, labels, tier_index, template):
    sums = jax.ops.segment_sum(series.T.astype(jnp.float32), labels, num_segments=PARCELS).T
    counts = jax.ops.segment_sum(jnp.ones((GRAY,), jnp.float32), labels, num_segments=PARCELS)
    means = sums / jnp.maximum(counts, 1.0)[None, :]
    parcel_z = standardize(means).astype(jnp.bfloat16)
    offsets = (jnp.arange(TIER, dtype=jnp.int32) // TIER_DEV * GRAY_DEV).astype(jnp.int32)
    picked = jnp.take(series, (tier_index + offsets).astype(jnp.int32), axis=1).astype(jnp.float32)
    vertex_z = standardize(picked).astype(jnp.bfloat16)
    profiles = (lax.dot_general(vertex_z, parcel_z, (((0,), (0,)), ((), ())), preferred_element_type=jnp.float32) / jnp.sqrt(jnp.float32(FRAMES))).astype(jnp.bfloat16)
    cross = lax.dot_general(profiles, template, (((0,), (0,)), ((), ())), preferred_element_type=jnp.float32)
    iterate = cross / jnp.sqrt(jnp.sum(cross * cross) + 1e-06)
    for step in range(NS_STEPS):
        inner = jnp.dot(iterate, iterate.T, precision=lax.Precision.HIGHEST)
        iterate = 1.5 * iterate - 0.5 * jnp.dot(inner, iterate, precision=lax.Precision.HIGHEST)
    rotation = iterate * jnp.sqrt(jnp.float32(PARCELS))
    return (profiles, rotation)
```

```python
import functools

import jax
import jax.numpy as jnp
import numpy as np
from jax import lax
from jax.experimental import pallas as pl
from jax.experimental.pallas import tpu as pltpu
from jax.sharding import PartitionSpec as P

NS_STEPS = 4
NX, NZ, NC = 4, 8, 2
PLANE = NX * NZ * NC
GROUP = NX * NC
MESH = pl.DeviceIdType.MESH
NT = (((1,), (1,)), ((), ()))
NN = (((1,), (0,)), ((), ()))
CORE = (0, 0, 1)
XS = [(dx, 0, 0) for dx in range(1, NX)]
ZS = [(0, dz, 0) for dz in range(1, NZ)]
DIAGONAL = [(dx, 0, 1) for dx in range(1, NX)]


def dot(a, b, dims):
    return lax.dot_general(a, b, dims, preferred_element_type=jnp.float32)


def standardize_rows(block):
    centered = block - jnp.mean(block, axis=1, keepdims=True)
    return centered / jnp.sqrt(jnp.mean(centered * centered, axis=1, keepdims=True) + 1e-05)


def exchange_kernel(
    split,
    n_sems,
    series_hbm,
    labels_ref,
    tier_ref,
    template_hbm,
    xg_ref,
    own_ref,
    norm_ref,
    po_ref,
    series,
    onehot,
    part,
    part_in,
    mine,
    a_in,
    b_in,
    a_sum,
    b_sum,
    a_in2,
    b_in2,
    cnt_out,
    cnt_in,
    cnt_mine,
    cnt_xin,
    cnt_x,
    cnt_zin,
    vz,
    tm,
    pz,
    pg,
    cx,
    cx_in,
    norm_part,
    norm_zin,
    norm_z,
    norm_xin,
    norm_x,
    norm_cin,
    send_sems,
    recv_sems,
    local_sems,
):
    frames, gray = series.shape
    parcels = cx.shape[2]
    rows = cx.shape[1]
    chunk = NZ * rows
    tier = vz.shape[1]
    me = lax.axis_index("vert")
    c = lax.rem(me, NC)
    z = lax.rem(me // NC, NZ)
    x = me // (NC * NZ)
    member = x * NC + c

    def x_at(dx):
        return lax.rem(x + dx + NX, NX)

    def z_at(dz):
        return lax.rem(z + dz + NZ, NZ)

    def device(offset):
        dx, dz, dc = offset
        return {"vert": (x_at(dx) * NZ + z_at(dz)) * NC + lax.rem(c + dc, NC)}

    counter = [0]
    pending = []

    def send(src, dst, offset):
        k = counter[0]
        counter[0] += 1
        copy = pltpu.make_async_remote_copy(
            src_ref=src,
            dst_ref=dst,
            send_sem=send_sems.at[k],
            recv_sem=recv_sems.at[k],
            device_id=device(offset),
            device_id_type=MESH,
        )
        copy.start()
        pending.append(copy)
        return copy

    series_copy = pltpu.make_async_copy(series_hbm, series, local_sems.at[0])
    series_copy.start()
    template_copy = pltpu.make_async_copy(template_hbm, tm.at[member], local_sems.at[1])
    template_copy.start()

    barrier = pltpu.get_barrier_semaphore()
    peers = [CORE] + XS + DIAGONAL + ZS
    for offset in peers:
        pl.semaphore_signal(barrier, inc=1, device_id=device(offset), device_id_type=MESH)

    half = parcels // NC

    def fill_onehot(side, core):
        q = lax.broadcasted_iota(jnp.int32, (half, gray), 0)
        parcel = ((q // rows) * NC + core) * rows + q % rows
        onehot[side] = (parcel == labels_ref[...]).astype(jnp.bfloat16)

    fill_onehot(0, 1 - c)
    series_copy.wait()
    pl.semaphore_wait(barrier, len(peers))

    spans = [(split, frames), (0, split)]
    core_sends = []
    for lo, hi in spans:
        block = dot(onehot[0], series[lo:hi, :], NT)
        part[:, :, :, lo:hi] = block.reshape(NX, NZ, rows, hi - lo)
        core_sends.append(send(part.at[:, :, :, lo:hi], part_in.at[:, :, :, lo:hi], CORE))
    fill_onehot(1, c)
    a_sends, b_sends = [], []
    for n, (lo, hi) in enumerate(spans):
        block = dot(onehot[1], series[lo:hi, :], NT).reshape(NX, NZ, rows, hi - lo)
        core_sends[n].wait_recv()
        mine[:, :, :, lo:hi] = block + part_in[:, :, :, lo:hi]
        if n == 0:
            for k, offset in enumerate(ZS):
                b_sends.append(send(mine.at[:, z_at(k + 1), :, lo:hi], b_in.at[k], offset))
        else:
            for k, offset in enumerate(XS):
                a_sends.append(send(mine.at[x_at(k + 1), :, :, lo:hi], a_in.at[k], offset))

    ones = jnp.ones((8, gray), jnp.bfloat16)
    away = dot(ones, onehot[0], NT)
    for k in range(NX):
        cnt_out[k] = away[:, k * chunk : (k + 1) * chunk]
    cnt_core = send(cnt_out, cnt_in, CORE)
    home = dot(ones, onehot[1], NT)

    ids = jnp.broadcast_to(tier_ref[...].astype(jnp.float32), (tier, tier))
    diagonal = lax.broadcasted_iota(jnp.int32, (tier, tier), 0) == lax.broadcasted_iota(
        jnp.int32, (tier, tier), 1
    )
    column = jnp.sum(jnp.where(diagonal, ids, 0.0), axis=1, keepdims=True).astype(jnp.int32)
    pick = (column == lax.broadcasted_iota(jnp.int32, (tier, gray), 1)).astype(jnp.bfloat16)
    vz[member] = standardize_rows(dot(pick, series[...], NT)).astype(jnp.bfloat16)

    cnt_core.wait_recv()
    for k in range(NX):
        cnt_mine[k] = home[:, k * chunk : (k + 1) * chunk] + cnt_in[k]
    cnt_x_sends = [
        send(cnt_mine.at[x_at(k + 1)], cnt_xin.at[k], offset) for k, offset in enumerate(XS)
    ]
    vz_sends = [send(vz.at[member], vz.at[member], CORE)]
    template_copy.wait()
    tm_sends = [send(tm.at[member], tm.at[member], CORE)]

    for copy in b_sends:
        copy.wait_recv()
    total = mine[:, z, :, split:]
    for k in range(NZ - 1):
        total = total + b_in[k]
    b_sum[...] = total
    b_sends2 = [send(b_sum.at[x_at(k + 1)], b_in2.at[k], offset) for k, offset in enumerate(XS)]
    for copy in cnt_x_sends:
        copy.wait_recv()
    cnt_x[...] = cnt_mine[x] + cnt_xin[0] + cnt_xin[1] + cnt_xin[2]
    cnt_z_sends = [send(cnt_x, cnt_zin.at[k], offset) for k, offset in enumerate(ZS)]
    for copy in a_sends:
        copy.wait_recv()
    a_sum[...] = mine[x, :, :, :split] + a_in[0] + a_in[1] + a_in[2]
    a_sends2 = [send(a_sum.at[z_at(k + 1)], a_in2.at[k], offset) for k, offset in enumerate(ZS)]

    vz_x = [send(vz.at[member], vz.at[member], offset) for offset in XS]
    tm_x = [send(tm.at[member], tm.at[member], offset) for offset in XS]

    for copy in b_sends2 + cnt_z_sends + a_sends2:
        copy.wait_recv()
    a_total = a_sum[z]
    for k in range(NZ - 1):
        a_total = a_total + a_in2[k]
    b_total = b_sum[x] + b_in2[0] + b_in2[1] + b_in2[2]
    counts = cnt_x[...]
    for k in range(NZ - 1):
        counts = counts + cnt_zin[k]
    spot = lax.broadcasted_iota(jnp.int32, (rows, chunk), 1) == z * rows + lax.broadcasted_iota(
        jnp.int32, (rows, chunk), 0
    )
    counts = jnp.concatenate([counts] * (rows // 8), axis=0)
    count = jnp.sum(jnp.where(spot, counts, 0.0), axis=1, keepdims=True)
    sums = jnp.concatenate([a_total, b_total], axis=1)
    pz[z] = standardize_rows(sums / jnp.maximum(count, 1.0)).astype(jnp.bfloat16)
    pz_sends = [send(pz.at[z], pz.at[z], offset) for offset in ZS]

    for sends, held, onward in ((vz_x, vz, vz_sends), (tm_x, tm, tm_sends)):
        for k, copy in enumerate(sends):
            copy.wait_recv()
            owner = x_at(-(k + 1)) * NC + c
            onward.append(send(held.at[owner], held.at[owner], CORE))
    for copy in pz_sends + vz_sends + tm_sends:
        copy.wait_recv()

    scale = np.float32(1.0 / np.sqrt(frames))
    pzs = pz[...].reshape(chunk, frames)
    vzs = vz[...].reshape(GROUP * tier, frames)
    turned = (dot(pzs, vzs, NT) * scale).astype(jnp.bfloat16)
    cx[...] = dot(turned, tm[...].reshape(GROUP * tier, parcels), NN).reshape(NZ, rows, parcels)
    cx_sends = [send(cx.at[z_at(k + 1)], cx_in.at[k], offset) for k, offset in enumerate(ZS)]

    pg[...] = (dot(vzs, pzs, NT) * scale).astype(jnp.bfloat16).reshape(GROUP, tier, chunk)
    po_ref[member] = pg[member]
    po_sends = []
    for dx, _, dc in [CORE] + XS + DIAGONAL:
        owner = x_at(dx) * NC + lax.rem(c + dc, NC)
        po_sends.append(send(pg.at[owner], po_ref.at[member], (dx, 0, dc)))

    for copy in cx_sends:
        copy.wait_recv()
    cross = cx[z]
    for k in range(NZ - 1):
        cross = cross + cx_in[k]
    own_ref[...] = cross
    xg_ref[x, z, c] = cross.astype(jnp.bfloat16)
    xg_z = [send(xg_ref.at[x, z, c], xg_ref.at[x, z, c], offset) for offset in ZS]
    square = jnp.sum(jnp.sum(cross * cross, axis=1, keepdims=True), axis=0, keepdims=True)
    norm_part[...] = jnp.broadcast_to(square, norm_part.shape)
    norm_zs = [send(norm_part, norm_zin.at[k], offset) for k, offset in enumerate(ZS)]
    for copy in xg_z + norm_zs:
        copy.wait_recv()
    xg_x = [send(xg_ref.at[x, :, c], xg_ref.at[x, :, c], offset) for offset in XS]
    norm = norm_part[...]
    for k in range(NZ - 1):
        norm = norm + norm_zin[k]
    norm_z[...] = norm
    norm_xs = [send(norm_z, norm_xin.at[k], offset) for k, offset in enumerate(XS)]
    xg_c = [send(xg_ref.at[x, :, c], xg_ref.at[x, :, c], CORE)]
    for copy in norm_xs:
        copy.wait_recv()
    norm_x[...] = norm_z[...] + norm_xin[0] + norm_xin[1] + norm_xin[2]
    norm_core = send(norm_x, norm_cin, CORE)
    for k, copy in enumerate(xg_x):
        copy.wait_recv()
        there = x_at(-(k + 1))
        xg_c.append(send(xg_ref.at[there, :, c], xg_ref.at[there, :, c], CORE))
    norm_core.wait_recv()
    norm_ref[...] = norm_x[...] + norm_cin[...]
    for copy in xg_c + po_sends:
        copy.wait_recv()
    for copy in pending:
        copy.wait_send()
    assert counter[0] == n_sems


def polar_kernel(xg_ref, own_ref, norm_ref, po_ref, profiles_ref, rotation_ref, full, rounded):
    parcels = full.shape[0]
    rows = own_ref.shape[0]
    chunk = po_ref.shape[2]
    scale = 1.0 / jnp.sqrt(norm_ref[0:1, 0:1] + 1e-06)
    full[...] = xg_ref[...].astype(jnp.float32) * scale
    current = own_ref[...] * scale

    wide = NC * chunk
    old = lax.broadcasted_iota(jnp.int32, (wide, wide), 0)
    new = lax.broadcasted_iota(jnp.int32, (wide, wide), 1)
    target = (((old % chunk) // rows) * NC + old // chunk) * rows + old % rows
    order = (target == new).astype(jnp.bfloat16)
    for k in range(NX):
        pair = jnp.concatenate([po_ref[NC * k + n] for n in range(NC)], axis=1)
        profiles_ref[:, k * wide : (k + 1) * wide] = dot(pair, order, NN).astype(jnp.bfloat16)

    for step in range(NS_STEPS):
        rounded[...] = full[...].astype(jnp.bfloat16)
        if step < NS_STEPS - 1:
            inner = dot(rounded[...], rounded[...], NT).astype(jnp.bfloat16)
            full[...] = 1.5 * full[...] - 0.5 * dot(inner, rounded[...], NN)
        high = current.astype(jnp.bfloat16)
        low = (current - high.astype(jnp.float32)).astype(jnp.bfloat16)
        gram = dot(jnp.concatenate([high, low], axis=0), rounded[...], NT)
        gram = gram[:rows] + gram[rows:]
        high = gram.astype(jnp.bfloat16)
        low = (gram - high.astype(jnp.float32)).astype(jnp.bfloat16)
        product = dot(jnp.concatenate([high, low], axis=0), rounded[...], NN)
        current = 1.5 * current - 0.5 * (product[:rows] + product[rows:])
    rotation_ref[...] = current * jnp.sqrt(jnp.float32(parcels))


def local(series, labels, tier_index, template):
    frames, gray = series.shape
    tier, parcels = template.shape
    rows = parcels // PLANE
    chunk = NZ * rows
    split = frames // 8 * 5 // 128 * 128
    rest = frames - split
    f32, bf16 = jnp.float32, jnp.bfloat16
    n_sems = 93
    vmem = pl.BlockSpec(memory_space=pltpu.VMEM)
    hbm = pl.BlockSpec(memory_space=pl.ANY)
    xg, own, norm, po = pl.pallas_call(
        functools.partial(exchange_kernel, split, n_sems),
        out_shape=(
            jax.ShapeDtypeStruct((NX, NZ, NC, rows, parcels), bf16),
            jax.ShapeDtypeStruct((rows, parcels), f32),
            jax.ShapeDtypeStruct((8, 128), f32),
            jax.ShapeDtypeStruct((GROUP, tier, chunk), bf16),
        ),
        in_specs=[hbm, vmem, vmem, hbm],
        out_specs=(vmem,) * 4,
        scratch_shapes=[
            pltpu.VMEM((frames, gray), bf16),
            pltpu.VMEM((NC, parcels // NC, gray), bf16),
            pltpu.VMEM((NX, NZ, rows, frames), f32),
            pltpu.VMEM((NX, NZ, rows, frames), f32),
            pltpu.VMEM((NX, NZ, rows, frames), f32),
            pltpu.VMEM((NX - 1, NZ, rows, split), f32),
            pltpu.VMEM((NZ - 1, NX, rows, rest), f32),
            pltpu.VMEM((NZ, rows, split), f32),
            pltpu.VMEM((NX, rows, rest), f32),
            pltpu.VMEM((NZ - 1, rows, split), f32),
            pltpu.VMEM((NX - 1, rows, rest), f32),
            pltpu.VMEM((NX, 8, chunk), f32),
            pltpu.VMEM((NX, 8, chunk), f32),
            pltpu.VMEM((NX, 8, chunk), f32),
            pltpu.VMEM((NX - 1, 8, chunk), f32),
            pltpu.VMEM((8, chunk), f32),
            pltpu.VMEM((NZ - 1, 8, chunk), f32),
            pltpu.VMEM((GROUP, tier, frames), bf16),
            pltpu.VMEM((GROUP, tier, parcels), bf16),
            pltpu.VMEM((NZ, rows, frames), bf16),
            pltpu.VMEM((GROUP, tier, chunk), bf16),
            pltpu.VMEM((NZ, rows, parcels), f32),
            pltpu.VMEM((NZ - 1, rows, parcels), f32),
            pltpu.VMEM((8, 128), f32),
            pltpu.VMEM((NZ - 1, 8, 128), f32),
            pltpu.VMEM((8, 128), f32),
            pltpu.VMEM((NX - 1, 8, 128), f32),
            pltpu.VMEM((8, 128), f32),
            pltpu.VMEM((8, 128), f32),
            pltpu.SemaphoreType.DMA((n_sems,)),
            pltpu.SemaphoreType.DMA((n_sems,)),
            pltpu.SemaphoreType.DMA((2,)),
        ],
        compiler_params=pltpu.CompilerParams(
            collective_id=0, has_side_effects=True, vmem_limit_bytes=56 * 2**20
        ),
        name="exchange",
    )(series, labels.reshape(1, gray), tier_index.reshape(1, tier), template)
    return pl.pallas_call(
        polar_kernel,
        out_shape=(
            jax.ShapeDtypeStruct((tier, parcels), bf16),
            jax.ShapeDtypeStruct((rows, parcels), f32),
        ),
        in_specs=[vmem] * 4,
        out_specs=(vmem,) * 2,
        scratch_shapes=[
            pltpu.VMEM((parcels, parcels), f32),
            pltpu.VMEM((parcels, parcels), bf16),
        ],
        compiler_params=pltpu.CompilerParams(vmem_limit_bytes=56 * 2**20),
        name="polar",
    )(xg.reshape(parcels, parcels), own, norm, po)


def solution(mesh):
    placed = (P("subj", "vert"), P("vert"), P("vert"), P("vert", None))
    return jax.shard_map(
        local,
        mesh=mesh,
        in_specs=placed,
        out_specs=(P("vert", "subj"), P("vert", "subj")),
        check_vma=False,
    )
```

```python
import functools

import jax
import jax.numpy as jnp
import numpy as np
from jax import lax
from jax.experimental import pallas as pl
from jax.experimental.pallas import tpu as pltpu
from jax.sharding import PartitionSpec as P

NS_STEPS = 4
NX, NZ, NC = 4, 8, 2
PLANE = NX * NZ * NC
GROUP = NX * NC
MESH = pl.DeviceIdType.MESH
NT = (((1,), (1,)), ((), ()))
NN = (((1,), (0,)), ((), ()))
CORE = (0, 0, 1)
XS = [(dx, 0, 0) for dx in range(1, NX)]
ZS = [(0, dz, 0) for dz in range(1, NZ)]
BESIDE = [(1, 0, 0), (NX - 1, 0, 0)]
DIAGONAL = [(dx, 0, 1) for dx in range(1, NX)]


def dot(a, b, dims):
    return lax.dot_general(a, b, dims, preferred_element_type=jnp.float32)


def standardize_rows(block):
    centered = block - jnp.mean(block, axis=1, keepdims=True)
    return centered / jnp.sqrt(jnp.mean(centered * centered, axis=1, keepdims=True) + 1e-05)


def exchange_kernel(
    split,
    n_sems,
    series_hbm,
    labels_ref,
    tier_ref,
    template_hbm,
    xg_ref,
    own_ref,
    norm_ref,
    po_ref,
    series,
    onehot,
    part,
    part_in,
    mine,
    a_in,
    b_in,
    a_sum,
    b_sum,
    a_in2,
    b_in2,
    cnt_out,
    cnt_in,
    cnt_mine,
    cnt_xin,
    cnt_x,
    cnt_zin,
    vz,
    tm,
    pz,
    pg,
    cx,
    cx_in,
    norm_part,
    norm_zin,
    norm_z,
    norm_xin,
    norm_x,
    norm_cin,
    send_sems,
    recv_sems,
    local_sems,
):
    frames, gray = series.shape
    parcels = cx.shape[2]
    rows = cx.shape[1]
    chunk = NZ * rows
    tier = vz.shape[1]
    me = lax.axis_index("vert")
    c = lax.rem(me, NC)
    z = lax.rem(me // NC, NZ)
    x = me // (NC * NZ)
    member = x * NC + c

    def x_at(dx):
        return lax.rem(x + dx + NX, NX)

    def z_at(dz):
        return lax.rem(z + dz + NZ, NZ)

    def device(offset):
        dx, dz, dc = offset
        return {"vert": (x_at(dx) * NZ + z_at(dz)) * NC + lax.rem(c + dc, NC)}

    counter = [0]
    pending = []

    def send(src, dst, offset):
        k = counter[0]
        counter[0] += 1
        copy = pltpu.make_async_remote_copy(
            src_ref=src,
            dst_ref=dst,
            send_sem=send_sems.at[k],
            recv_sem=recv_sems.at[k],
            device_id=device(offset),
            device_id_type=MESH,
        )
        copy.start()
        pending.append(copy)
        return copy

    series_copy = pltpu.make_async_copy(series_hbm, series, local_sems.at[0])
    series_copy.start()
    template_copy = pltpu.make_async_copy(template_hbm, tm.at[member], local_sems.at[1])
    template_copy.start()

    barrier = pltpu.get_barrier_semaphore()
    peers = [CORE] + XS + DIAGONAL + ZS
    for offset in peers:
        pl.semaphore_signal(barrier, inc=1, device_id=device(offset), device_id_type=MESH)

    half = parcels // NC

    def fill_onehot(side, core):
        q = lax.broadcasted_iota(jnp.int32, (half, gray), 0)
        parcel = ((q // rows) * NC + core) * rows + q % rows
        onehot[side] = (parcel == labels_ref[...].reshape(1, gray)).astype(jnp.bfloat16)

    fill_onehot(0, 1 - c)
    series_copy.wait()
    pl.semaphore_wait(barrier, len(peers))

    template_copy.wait()
    tm_hop = [send(tm.at[member], tm.at[member], offset) for offset in BESIDE]

    spans = [(split, frames), (0, split)]
    core_sends = []
    for lo, hi in spans:
        block = dot(onehot[0], series[lo:hi, :], NT)
        part[:, :, :, lo:hi] = block.reshape(NX, NZ, rows, hi - lo)
        core_sends.append(send(part.at[:, :, :, lo:hi], part_in.at[:, :, :, lo:hi], CORE))
    fill_onehot(1, c)
    a_sends, b_sends = [], []
    for n, (lo, hi) in enumerate(spans):
        block = dot(onehot[1], series[lo:hi, :], NT).reshape(NX, NZ, rows, hi - lo)
        core_sends[n].wait_recv()
        mine[:, :, :, lo:hi] = block + part_in[:, :, :, lo:hi]
        if n == 0:
            for k, offset in enumerate(ZS):
                b_sends.append(send(mine.at[:, z_at(k + 1), :, lo:hi], b_in.at[k], offset))
        else:
            for k, offset in enumerate(XS):
                a_sends.append(send(mine.at[x_at(k + 1), :, :, lo:hi], a_in.at[k], offset))

    ones = jnp.ones((8, gray), jnp.bfloat16)
    away = dot(ones, onehot[0], NT)
    for k in range(NX):
        cnt_out[k] = away[:, k * chunk : (k + 1) * chunk]
    cnt_core = send(cnt_out, cnt_in, CORE)
    home = dot(ones, onehot[1], NT)

    ids = jnp.broadcast_to(tier_ref[...].reshape(1, tier).astype(jnp.float32), (tier, tier))
    diagonal = lax.broadcasted_iota(jnp.int32, (tier, tier), 0) == lax.broadcasted_iota(
        jnp.int32, (tier, tier), 1
    )
    column = jnp.sum(jnp.where(diagonal, ids, 0.0), axis=1, keepdims=True).astype(jnp.int32)
    pick = (column == lax.broadcasted_iota(jnp.int32, (tier, gray), 1)).astype(jnp.bfloat16)
    vz[member] = standardize_rows(dot(pick, series[...], NT)).astype(jnp.bfloat16)

    cnt_core.wait_recv()
    for k in range(NX):
        cnt_mine[k] = home[:, k * chunk : (k + 1) * chunk] + cnt_in[k]
    cnt_x_sends = [
        send(cnt_mine.at[x_at(k + 1)], cnt_xin.at[k], offset) for k, offset in enumerate(XS)
    ]
    vz_sends = [send(vz.at[member], vz.at[member], CORE)]
    tm_sends = [send(tm.at[member], tm.at[member], CORE)]

    for copy in b_sends:
        copy.wait_recv()
    total = mine[:, z, :, split:]
    for k in range(NZ - 1):
        total = total + b_in[k]
    b_sum[...] = total
    b_sends2 = [send(b_sum.at[x_at(k + 1)], b_in2.at[k], offset) for k, offset in enumerate(XS)]
    for copy in cnt_x_sends:
        copy.wait_recv()
    cnt_x[...] = cnt_mine[x] + cnt_xin[0] + cnt_xin[1] + cnt_xin[2]
    cnt_z_sends = [send(cnt_x, cnt_zin.at[k], offset) for k, offset in enumerate(ZS)]
    for copy in a_sends:
        copy.wait_recv()
    a_sum[...] = mine[x, :, :, :split] + a_in[0] + a_in[1] + a_in[2]
    a_sends2 = [send(a_sum.at[z_at(k + 1)], a_in2.at[k], offset) for k, offset in enumerate(ZS)]

    vz_hop = [send(vz.at[member], vz.at[member], offset) for offset in BESIDE]
    front, back = pl.ds(0, tier // 2), pl.ds(tier // 2, tier // 2)
    left, right = x_at(-1) * NC + c, x_at(1) * NC + c
    opposite = x_at(2) * NC + c

    def second_hop(hop, held, onward):
        for copy in hop:
            copy.wait_recv()
        onward += [send(held.at[owner], held.at[owner], CORE) for owner in (left, right)]
        return [
            send(held.at[left, front], held.at[left, front], BESIDE[0]),
            send(held.at[right, back], held.at[right, back], BESIDE[1]),
        ]

    def pass_opposite(hop, held, onward):
        for copy in hop:
            copy.wait_recv()
        onward.append(send(held.at[opposite], held.at[opposite], CORE))

    vz_hop2 = second_hop(vz_hop, vz, vz_sends)
    tm_hop2 = second_hop(tm_hop, tm, tm_sends)

    for copy in b_sends2 + cnt_z_sends + a_sends2:
        copy.wait_recv()
    a_total = a_sum[z]
    for k in range(NZ - 1):
        a_total = a_total + a_in2[k]
    b_total = b_sum[x] + b_in2[0] + b_in2[1] + b_in2[2]
    counts = cnt_x[...]
    for k in range(NZ - 1):
        counts = counts + cnt_zin[k]
    spot = lax.broadcasted_iota(jnp.int32, (rows, chunk), 1) == z * rows + lax.broadcasted_iota(
        jnp.int32, (rows, chunk), 0
    )
    counts = jnp.concatenate([counts] * (rows // 8), axis=0)
    count = jnp.sum(jnp.where(spot, counts, 0.0), axis=1, keepdims=True)
    sums = jnp.concatenate([a_total, b_total], axis=1)
    pz[z] = standardize_rows(sums / jnp.maximum(count, 1.0)).astype(jnp.bfloat16)
    pz_sends = [send(pz.at[z], pz.at[z], offset) for offset in ZS]

    pass_opposite(vz_hop2, vz, vz_sends)
    pass_opposite(tm_hop2, tm, tm_sends)
    for copy in pz_sends + vz_sends + tm_sends:
        copy.wait_recv()

    scale = np.float32(1.0 / np.sqrt(frames))
    pzs = pz[...].reshape(chunk, frames)
    vzs = vz[...].reshape(GROUP * tier, frames)
    turned = (dot(pzs, vzs, NT) * scale).astype(jnp.bfloat16)
    cx[...] = dot(turned, tm[...].reshape(GROUP * tier, parcels), NN).reshape(NZ, rows, parcels)
    cx_sends = [send(cx.at[z_at(k + 1)], cx_in.at[k], offset) for k, offset in enumerate(ZS)]

    pg[...] = (dot(vzs, pzs, NT) * scale).astype(jnp.bfloat16).reshape(GROUP, tier, chunk)
    po_ref[member] = pg[member]
    po_sends = []
    for dx, _, dc in [CORE] + XS + DIAGONAL:
        owner = x_at(dx) * NC + lax.rem(c + dc, NC)
        po_sends.append(send(pg.at[owner], po_ref.at[member], (dx, 0, dc)))

    for copy in cx_sends:
        copy.wait_recv()
    cross = cx[z]
    for k in range(NZ - 1):
        cross = cross + cx_in[k]
    own_ref[...] = cross
    xg_ref[x, z, c] = cross.astype(jnp.bfloat16)
    square = jnp.sum(jnp.sum(cross * cross, axis=1, keepdims=True), axis=0, keepdims=True)
    norm_part[...] = jnp.broadcast_to(square, norm_part.shape)

    def spread(at_x, at_z, offsets):
        block = xg_ref.at[at_x, at_z, c]
        return [send(block, block, offset) for offset in offsets]

    xg_z = spread(x, z, ZS)
    norm_zs = [send(norm_part, norm_zin.at[k], offset) for k, offset in enumerate(ZS)]
    xg_x = [(z, spread(x, z, XS))]
    xg_c = spread(x, z, [CORE])
    norm = norm_part[...]
    near_first = sorted(range(1, NZ), key=lambda dz: min(dz, NZ - dz))
    for dz in near_first:
        xg_z[dz - 1].wait_recv()
        there = z_at(-dz)
        xg_x.append((there, spread(x, there, XS)))
        xg_c += spread(x, there, [CORE])
    for copy in norm_zs:
        copy.wait_recv()
    for k in range(NZ - 1):
        norm = norm + norm_zin[k]
    norm_z[...] = norm
    norm_xs = [send(norm_z, norm_xin.at[k], offset) for k, offset in enumerate(XS)]
    norm_core = None
    for n, (there, copies) in enumerate(xg_x):
        for k, copy in enumerate(copies):
            copy.wait_recv()
            xg_c += spread(x_at(-(k + 1)), there, [CORE])
        if n == 4:
            for copy in norm_xs:
                copy.wait_recv()
            norm_x[...] = norm_z[...] + norm_xin[0] + norm_xin[1] + norm_xin[2]
            norm_core = send(norm_x, norm_cin, CORE)
    norm_core.wait_recv()
    norm_ref[...] = norm_x[...] + norm_cin[...]
    for copy in xg_c + po_sends:
        copy.wait_recv()
    for copy in pending:
        copy.wait_send()
    assert counter[0] == n_sems


def polar_kernel(xg_ref, own_ref, norm_ref, po_ref, profiles_ref, rotation_ref, full, rounded, gram):
    parcels = full.shape[0]
    rows = own_ref.shape[0]
    chunk = po_ref.shape[2]
    block = parcels // 4
    own = pl.ds(pl.multiple_of(lax.axis_index("vert") * rows, rows), rows)
    scale = 1.0 / jnp.sqrt(norm_ref[0:1, 0:1] + 1e-06)
    full[...] = xg_ref[...].astype(jnp.float32) * scale
    full[own, :] = own_ref[...] * scale

    wide = NC * chunk
    old = lax.broadcasted_iota(jnp.int32, (wide, wide), 0)
    new = lax.broadcasted_iota(jnp.int32, (wide, wide), 1)
    target = (((old % chunk) // rows) * NC + old // chunk) * rows + old % rows
    order = (target == new).astype(jnp.bfloat16)
    for k in range(NX):
        pair = jnp.concatenate([po_ref[NC * k + n] for n in range(NC)], axis=1)
        profiles_ref[:, k * wide : (k + 1) * wide] = dot(pair, order, NN).astype(jnp.bfloat16)

    def thin(values, matrix, dims):
        high = values.astype(jnp.bfloat16)
        low = (values - high.astype(jnp.float32)).astype(jnp.bfloat16)
        product = dot(jnp.concatenate([high, low], axis=0), matrix[...], dims)
        return product[:rows] + product[rows:]

    for step in range(NS_STEPS):
        rounded[...] = full[...].astype(jnp.bfloat16)
        if step == NS_STEPS - 1:
            break
        for lo in range(0, parcels, block):
            hi = lo + block
            piece = dot(rounded[lo:, :], rounded[lo:hi, :], NT)
            gram[lo:, lo:hi] = piece.astype(jnp.bfloat16)
            if hi < parcels:
                gram[lo:hi, hi:] = piece[block:].T.astype(jnp.bfloat16)
        full[...] = 1.5 * full[...] - 0.5 * dot(gram[...], rounded[...], NN)
    current = full[own, :]
    product = thin(thin(current, rounded, NT), rounded, NN)
    rotation_ref[...] = (1.5 * current - 0.5 * product) * jnp.sqrt(jnp.float32(parcels))


def local(series, labels, tier_index, template):
    frames, gray = series.shape
    tier, parcels = template.shape
    rows = parcels // PLANE
    chunk = NZ * rows
    split = frames // 8 * 5 // 128 * 128
    rest = frames - split
    f32, bf16 = jnp.float32, jnp.bfloat16
    n_sems = 144
    vmem = pl.BlockSpec(memory_space=pltpu.VMEM)
    hbm = pl.BlockSpec(memory_space=pl.ANY)
    xg, own, norm, po = pl.pallas_call(
        functools.partial(exchange_kernel, split, n_sems),
        out_shape=(
            jax.ShapeDtypeStruct((NX, NZ, NC, rows, parcels), bf16),
            jax.ShapeDtypeStruct((rows, parcels), f32),
            jax.ShapeDtypeStruct((8, 128), f32),
            jax.ShapeDtypeStruct((GROUP, tier, chunk), bf16),
        ),
        in_specs=[hbm, vmem, vmem, hbm],
        out_specs=(vmem,) * 4,
        scratch_shapes=[
            pltpu.VMEM((frames, gray), bf16),
            pltpu.VMEM((NC, parcels // NC, gray), bf16),
            pltpu.VMEM((NX, NZ, rows, frames), f32),
            pltpu.VMEM((NX, NZ, rows, frames), f32),
            pltpu.VMEM((NX, NZ, rows, frames), f32),
            pltpu.VMEM((NX - 1, NZ, rows, split), f32),
            pltpu.VMEM((NZ - 1, NX, rows, rest), f32),
            pltpu.VMEM((NZ, rows, split), f32),
            pltpu.VMEM((NX, rows, rest), f32),
            pltpu.VMEM((NZ - 1, rows, split), f32),
            pltpu.VMEM((NX - 1, rows, rest), f32),
            pltpu.VMEM((NX, 8, chunk), f32),
            pltpu.VMEM((NX, 8, chunk), f32),
            pltpu.VMEM((NX, 8, chunk), f32),
            pltpu.VMEM((NX - 1, 8, chunk), f32),
            pltpu.VMEM((8, chunk), f32),
            pltpu.VMEM((NZ - 1, 8, chunk), f32),
            pltpu.VMEM((GROUP, tier, frames), bf16),
            pltpu.VMEM((GROUP, tier, parcels), bf16),
            pltpu.VMEM((NZ, rows, frames), bf16),
            pltpu.VMEM((GROUP, tier, chunk), bf16),
            pltpu.VMEM((NZ, rows, parcels), f32),
            pltpu.VMEM((NZ - 1, rows, parcels), f32),
            pltpu.VMEM((8, 128), f32),
            pltpu.VMEM((NZ - 1, 8, 128), f32),
            pltpu.VMEM((8, 128), f32),
            pltpu.VMEM((NX - 1, 8, 128), f32),
            pltpu.VMEM((8, 128), f32),
            pltpu.VMEM((8, 128), f32),
            pltpu.SemaphoreType.DMA((n_sems,)),
            pltpu.SemaphoreType.DMA((n_sems,)),
            pltpu.SemaphoreType.DMA((2,)),
        ],
        compiler_params=pltpu.CompilerParams(
            collective_id=0, has_side_effects=True, vmem_limit_bytes=56 * 2**20
        ),
        name="exchange",
    )(series, labels, tier_index, template)
    return pl.pallas_call(
        polar_kernel,
        out_shape=(
            jax.ShapeDtypeStruct((tier, parcels), bf16),
            jax.ShapeDtypeStruct((rows, parcels), f32),
        ),
        in_specs=[vmem] * 4,
        out_specs=(vmem,) * 2,
        scratch_shapes=[
            pltpu.VMEM((parcels, parcels), f32),
            pltpu.VMEM((parcels, parcels), bf16),
            pltpu.VMEM((parcels, parcels), bf16),
        ],
        compiler_params=pltpu.CompilerParams(vmem_limit_bytes=56 * 2**20),
        name="polar",
    )(xg.reshape(parcels, parcels), own, norm, po)


def solution(mesh):
    placed = (P("subj", "vert"), P("vert"), P("vert"), P("vert", None))
    return jax.shard_map(
        local,
        mesh=mesh,
        in_specs=placed,
        out_specs=(P("vert", "subj"), P("vert", "subj")),
        check_vma=False,
    )
```

```python
import functools

import jax
import jax.numpy as jnp
import numpy as np
from jax import lax
from jax.experimental import pallas as pl
from jax.experimental.pallas import tpu as pltpu
from jax.sharding import PartitionSpec as P

NS_STEPS = 4
NX, NZ, NC = 4, 8, 2
PLANE = NX * NZ * NC
GROUP = NX * NC
MESH = pl.DeviceIdType.MESH
NPART = 2
NT = (((1,), (1,)), ((), ()))
NN = (((1,), (0,)), ((), ()))
CORE = (0, 0, 1)
XS = [(dx, 0, 0) for dx in range(1, NX)]
ZS = [(0, dz, 0) for dz in range(1, NZ)]
BESIDE = [(1, 0, 0), (NX - 1, 0, 0)]
DIAGONAL = [(dx, 0, 1) for dx in range(1, NX)]


def dot(a, b, dims):
    return lax.dot_general(a, b, dims, preferred_element_type=jnp.float32)


def standardize_rows(block):
    centered = block - jnp.mean(block, axis=1, keepdims=True)
    return centered / jnp.sqrt(jnp.mean(centered * centered, axis=1, keepdims=True) + 1e-05)


def exchange_kernel(
    split,
    n_sems,
    series_hbm,
    labels_ref,
    tier_ref,
    template_hbm,
    po,
    rotation_ref,
    series,
    onehot,
    part,
    part_in,
    mine,
    a_in,
    b_in,
    a_sum,
    b_sum,
    a_in2,
    b_in2,
    cnt_out,
    cnt_in,
    cnt_mine,
    cnt_xin,
    cnt_x,
    cnt_zin,
    vz,
    tm,
    pz,
    pg,
    cx,
    cx_in,
    norm_part,
    norm_zin,
    norm_z,
    norm_xin,
    norm_x,
    norm_cin,
    xg,
    own_rows,
    gram,
    gram16,
    step_sum,
    step16,
    send_sems,
    recv_sems,
    local_sems,
):
    frames, gray = series.shape
    rows = cx.shape[2]
    width = cx.shape[3]
    parcels = NPART * width
    chunk = NZ * rows
    tier = vz.shape[1]
    me = lax.axis_index("vert")
    c = lax.rem(me, NC)
    z = lax.rem(me // NC, NZ)
    x = me // (NC * NZ)
    member = x * NC + c

    def x_at(dx):
        return lax.rem(x + dx + NX, NX)

    def z_at(dz):
        return lax.rem(z + dz + NZ, NZ)

    def device(offset):
        dx, dz, dc = offset
        return {"vert": (x_at(dx) * NZ + z_at(dz)) * NC + lax.rem(c + dc, NC)}

    groups = []

    class Group:
        def __init__(self, sized):
            self.sized = sized
            self.k = len(groups)
            groups.append(self)

        def send(self, src, dst, offset):
            pltpu.make_async_remote_copy(
                src_ref=src,
                dst_ref=dst,
                send_sem=send_sems.at[self.k],
                recv_sem=recv_sems.at[self.k],
                device_id=device(offset),
                device_id_type=MESH,
            ).start()

        def wait(self, sems):
            pltpu.make_async_copy(self.sized, self.sized, sems.at[self.k]).wait()

        def wait_recv(self):
            self.wait(recv_sems)

    def exchange(src, dst, offset):
        group = Group(dst)
        group.send(src, dst, offset)
        return group

    def scatter(pick, dst, offsets):
        group = Group(dst)
        for k, offset in enumerate(offsets):
            group.send(pick(k + 1), dst.at[k], offset)
        return group

    def repeat(block, sized, offsets):
        group = Group(sized)
        for offset in offsets:
            group.send(block, block, offset)
        return group

    series_copy = pltpu.make_async_copy(series_hbm, series, local_sems.at[0])
    series_copy.start()
    template_copy = pltpu.make_async_copy(template_hbm, tm.at[member], local_sems.at[1])
    template_copy.start()

    barrier = pltpu.get_barrier_semaphore()
    peers = [CORE] + XS + DIAGONAL + ZS
    for offset in peers:
        pl.semaphore_signal(barrier, inc=1, device_id=device(offset), device_id_type=MESH)

    half = parcels // NC

    def fill_onehot(side, core):
        q = lax.broadcasted_iota(jnp.int32, (half, gray), 0)
        parcel = ((q // rows) * NC + core) * rows + q % rows
        onehot[side] = (parcel == labels_ref[...].reshape(1, gray)).astype(jnp.bfloat16)

    fill_onehot(0, 1 - c)
    template_copy.wait()
    pl.semaphore_wait(barrier, len(peers))
    tm_hop = repeat(tm.at[member], tm.at[0:2], BESIDE)
    series_copy.wait()
    spans = [(split, frames), (0, split)]
    core_sends = []
    for lo, hi in spans:
        block = dot(onehot[0], series[lo:hi, :], NT)
        part[:, :, :, lo:hi] = block.reshape(NX, NZ, rows, hi - lo)
        core_sends.append(exchange(part.at[:, :, :, lo:hi], part_in.at[:, :, :, lo:hi], CORE))
    fill_onehot(1, c)
    for n, (lo, hi) in enumerate(spans):
        block = dot(onehot[1], series[lo:hi, :], NT).reshape(NX, NZ, rows, hi - lo)
        core_sends[n].wait_recv()
        mine[:, :, :, lo:hi] = block + part_in[:, :, :, lo:hi]
        if n == 0:
            b_group = scatter(lambda k: mine.at[:, z_at(k), :, lo:hi], b_in, ZS)
        else:
            a_near = Group(a_in.at[0:2])
            for dx in (1, NX - 1):
                a_near.send(mine.at[x_at(dx), :, :, lo:hi], a_in.at[dx - 1], (dx, 0, 0))
            a_far = exchange(mine.at[x_at(2), :, :, lo:hi], a_in.at[1], XS[1])

    ones = jnp.ones((8, gray), jnp.bfloat16)
    away = dot(ones, onehot[0], NT)
    for k in range(NX):
        cnt_out[k] = away[:, k * chunk : (k + 1) * chunk]
    cnt_core = exchange(cnt_out, cnt_in, CORE)
    home = dot(ones, onehot[1], NT)

    ids = jnp.broadcast_to(tier_ref[...].reshape(1, tier).astype(jnp.float32), (tier, tier))
    diagonal = lax.broadcasted_iota(jnp.int32, (tier, tier), 0) == lax.broadcasted_iota(
        jnp.int32, (tier, tier), 1
    )
    column = jnp.sum(jnp.where(diagonal, ids, 0.0), axis=1, keepdims=True).astype(jnp.int32)
    pick = (column == lax.broadcasted_iota(jnp.int32, (tier, gray), 1)).astype(jnp.bfloat16)
    vz[member] = standardize_rows(dot(pick, series[...], NT)).astype(jnp.bfloat16)

    cnt_core.wait_recv()
    for k in range(NX):
        cnt_mine[k] = home[:, k * chunk : (k + 1) * chunk] + cnt_in[k]
    cnt_xs = scatter(lambda k: cnt_mine.at[x_at(k)], cnt_xin, XS)

    def to_core(held):
        group = Group(held.at[0:NX])
        group.send(held.at[member], held.at[member], CORE)
        return group

    tm_core, vz_core = to_core(tm), to_core(vz)

    left, right = x_at(-1) * NC + c, x_at(1) * NC + c
    opposite = x_at(2) * NC + c
    front, back = pl.ds(0, tier // 2), pl.ds(tier // 2, tier // 2)

    def second_hop(hop, held, core):
        hop.wait_recv()
        group = Group(held.at[0])
        for owner, piece, offset in ((left, front, BESIDE[0]), (right, back, BESIDE[1])):
            group.send(held.at[owner, piece], held.at[owner, piece], offset)
            core.send(held.at[owner], held.at[owner], CORE)
        return group

    def pass_opposite(hop, held, core):
        hop.wait_recv()
        core.send(held.at[opposite], held.at[opposite], CORE)

    a_near.wait_recv()
    vz_hop = repeat(vz.at[member], vz.at[0:2], BESIDE)
    tm_hop2 = second_hop(tm_hop, tm, tm_core)
    a_far.wait_recv()
    a_sum[...] = mine[x, :, :, :split] + a_in[0] + a_in[1] + a_in[2]
    a_group2 = scatter(lambda k: a_sum.at[z_at(k)], a_in2, ZS)
    b_group.wait_recv()
    total = mine[:, z, :, split:]
    for k in range(NZ - 1):
        total = total + b_in[k]
    b_sum[...] = total
    b_group2 = scatter(lambda k: b_sum.at[x_at(k)], b_in2, XS)
    cnt_xs.wait_recv()
    cnt_x[...] = cnt_mine[x] + cnt_xin[0] + cnt_xin[1] + cnt_xin[2]
    cnt_zs = scatter(lambda k: cnt_x, cnt_zin, ZS)
    vz_hop2 = second_hop(vz_hop, vz, vz_core)

    for group in (b_group2, cnt_zs, a_group2):
        group.wait_recv()
    a_total = a_sum[z]
    for k in range(NZ - 1):
        a_total = a_total + a_in2[k]
    b_total = b_sum[x] + b_in2[0] + b_in2[1] + b_in2[2]
    counts = cnt_x[...]
    for k in range(NZ - 1):
        counts = counts + cnt_zin[k]
    spot = lax.broadcasted_iota(jnp.int32, (rows, chunk), 1) == z * rows + lax.broadcasted_iota(
        jnp.int32, (rows, chunk), 0
    )
    counts = jnp.concatenate([counts] * (rows // 8), axis=0)
    count = jnp.sum(jnp.where(spot, counts, 0.0), axis=1, keepdims=True)
    sums = jnp.concatenate([a_total, b_total], axis=1)
    pz[z] = standardize_rows(sums / jnp.maximum(count, 1.0)).astype(jnp.bfloat16)
    pz_group = repeat(pz.at[z], pz.at[0 : NZ - 1], ZS)
    pass_opposite(tm_hop2, tm, tm_core)
    pass_opposite(vz_hop2, vz, vz_core)
    for group in (vz_core, pz_group):
        group.wait_recv()

    scale = np.float32(1.0 / np.sqrt(frames))
    pzs = pz[...].reshape(chunk, frames)
    vzs = vz[...].reshape(GROUP * tier, frames)
    turned = (dot(pzs, vzs, NT) * scale).astype(jnp.bfloat16)
    tm_core.wait_recv()

    def scatter_cross(n):
        return scatter(lambda k: cx.at[n, z_at(k)], cx_in.at[n], ZS)

    cx_groups = []
    for n in range(NPART):
        columns = tm[:, :, n * width : (n + 1) * width].reshape(GROUP * tier, width)
        cx[n] = dot(turned, columns, NN).reshape(NZ, rows, width)
        cx_groups.append(scatter_cross(n))

    pg[...] = (dot(vzs, pzs, NT) * scale).astype(jnp.bfloat16).reshape(GROUP, tier, chunk)
    po[member] = pg[member]
    po_group = Group(po.at[0 : GROUP - 1])
    for dx, _, dc in [CORE] + XS + DIAGONAL:
        owner = x_at(dx) * NC + lax.rem(c + dc, NC)
        po_group.send(pg.at[owner], po.at[member], (dx, 0, dc))

    near_first = range(1, NZ // 2 + 1)
    xg_z, xg_x = [], [[] for _ in range(NPART)]
    xg_c = [Group(xg.at[n, :, :, 0]) for n in range(NPART)]

    def forward(n, at_z):
        block = xg.at[n, x, at_z, c]
        xg_x[n].append((at_z, repeat(block, xg.at[n, 0 : NX - 1, 0, 0], XS)))
        xg_c[n].send(block, block, CORE)

    def own_part(n):
        cx_groups[n].wait_recv()
        cross = cx[n, z]
        for k in range(NZ - 1):
            cross = cross + cx_in[n, k]
        own_rows[n] = cross
        xg[n, x, z, c] = cross.astype(jnp.bfloat16)
        block = xg.at[n, x, z, c]
        by_distance = []
        for dz in near_first:
            pair = [dz] if 2 * dz == NZ else [dz, NZ - dz]
            by_distance.append(
                (pair, repeat(block, xg.at[n, 0, 0 : len(pair), 0], [ZS[k - 1] for k in pair]))
            )
        xg_z.append(by_distance)
        forward(n, z)
        return jnp.sum(jnp.sum(cross * cross, axis=1, keepdims=True), axis=0, keepdims=True)

    def forward_z(n, distances):
        for pair, group in xg_z[n][distances]:
            group.wait_recv()
            for dz in pair:
                forward(n, z_at(-dz))

    square = own_part(0)
    for n in range(1, NPART):
        forward_z(n - 1, slice(0, 2))
        square = square + own_part(n)
        if n == NPART - 1:
            norm_part[...] = jnp.broadcast_to(square, norm_part.shape)
            norm_zs = scatter(lambda k: norm_part, norm_zin, ZS)
        forward_z(n - 1, slice(2, None))
    forward_z(NPART - 1, slice(0, None))
    norm_zs.wait_recv()
    norm = norm_part[...]
    for k in range(NZ - 1):
        norm = norm + norm_zin[k]
    norm_z[...] = norm
    norm_xs = scatter(lambda k: norm_z, norm_xin, XS)

    def pass_core(n, blocks):
        for at_z, group in blocks:
            group.wait_recv()
            for dx in range(1, NX):
                block = xg.at[n, x_at(dx), at_z, c]
                xg_c[n].send(block, block, CORE)

    square_block = parcels // 4
    edges = [(lo, lo + square_block) for lo in range(0, parcels, square_block)]

    def add_gram(n, lo, hi):
        rows_n = xg[n].reshape(parcels, width)
        piece = dot(rows_n[lo:], rows_n[lo:hi], NT)
        gram[lo:, lo:hi] = piece if n == 0 else gram[lo:, lo:hi] + piece

    for n in range(NPART):
        if n == 0:
            pass_core(0, xg_x[0])
        xg_c[n].wait_recv()
        for k, (lo, hi) in enumerate(edges):
            add_gram(n, lo, hi)
            if n + 1 < NPART:
                pass_core(n + 1, xg_x[n + 1][2 * k : 2 * k + 2])
            if n + 1 == NPART - 1 and k == 1:
                norm_xs.wait_recv()
                norm_x[...] = norm_z[...] + norm_xin[0] + norm_xin[1] + norm_xin[2]
                norm_core = exchange(norm_x, norm_cin, CORE)
    norm_core.wait_recv()
    total = norm_x[...] + norm_cin[...]
    unit = 1.0 / jnp.sqrt(total[0:1, 0:1] + 1e-06)

    def mirror(held, lo, hi, values):
        held[lo:, lo:hi] = values.astype(jnp.bfloat16)
        if hi < parcels:
            held[lo:hi, hi:] = values[hi - lo :].T.astype(jnp.bfloat16)

    def next_gram(old, new):
        for lo, hi in edges:
            values = 1.5 * gram[lo:, lo:hi] - 0.5 * dot(old[lo:, :], old[:, lo:hi], NN)
            step_sum[lo:, lo:hi] = values
            mirror(step16, lo, hi, values)
        for lo, hi in edges:
            values = 1.5 * step_sum[lo:, lo:hi] - 0.5 * dot(step16[lo:, :], old[:, lo:hi], NN)
            gram[lo:, lo:hi] = values
            mirror(new, lo, hi, values)

    def thin(values, matrix):
        high = values.astype(jnp.bfloat16)
        low = (values - high.astype(jnp.float32)).astype(jnp.bfloat16)
        product = dot(jnp.concatenate([high, low], axis=0), matrix, NN)
        return product[:rows] + product[rows:]

    def step_rows(values, held):
        return 1.5 * values - 0.5 * thin(values, held[...])

    for lo, hi in edges:
        values = gram[lo:, lo:hi] * (unit * unit)
        gram[lo:, lo:hi] = values
        mirror(gram16.at[0], lo, hi, values)
    identity = (
        lax.broadcasted_iota(jnp.int32, (rows, parcels), 1)
        == me * rows + lax.broadcasted_iota(jnp.int32, (rows, parcels), 0)
    ).astype(jnp.float32)
    factor = identity
    for step in range(NS_STEPS - 1):
        held = gram16.at[step % 2]
        factor = step_rows(factor, held)
        if step < NS_STEPS - 2:
            next_gram(held, gram16.at[(step + 1) % 2])
    product = step_rows(step_rows(thin(factor, held[...]), held), held)
    factor = 1.5 * factor - 0.5 * product
    linear = np.float32(1.5**NS_STEPS)
    rest = factor - linear * identity
    for n in range(NPART):
        out = linear * own_rows[n] + thin(rest, xg[n].reshape(parcels, width))
        rotation_ref[:, n * width : (n + 1) * width] = out * unit * jnp.sqrt(jnp.float32(parcels))
    po_group.wait_recv()
    for group in groups:
        group.wait(send_sems)
    assert len(groups) == n_sems


def finish_kernel(po_ref, rows_ref, profiles_ref, rotation_ref):
    chunk = po_ref.shape[2]
    rows = rows_ref.shape[0]
    rotation_ref[...] = rows_ref[...]
    wide = NC * chunk
    old = lax.broadcasted_iota(jnp.int32, (wide, wide), 0)
    new = lax.broadcasted_iota(jnp.int32, (wide, wide), 1)
    target = (((old % chunk) // rows) * NC + old // chunk) * rows + old % rows
    order = (target == new).astype(jnp.bfloat16)
    for k in range(NX):
        pair = jnp.concatenate([po_ref[NC * k + n] for n in range(NC)], axis=1)
        profiles_ref[:, k * wide : (k + 1) * wide] = dot(pair, order, NN).astype(jnp.bfloat16)


def local(series, labels, tier_index, template):
    frames, gray = series.shape
    tier, parcels = template.shape
    rows = parcels // PLANE
    chunk = NZ * rows
    width = parcels // NPART
    split = frames // 8 * 5 // 128 * 128
    rest = frames - split
    f32, bf16 = jnp.float32, jnp.bfloat16
    n_sems = 49
    vmem = pl.BlockSpec(memory_space=pltpu.VMEM)
    hbm = pl.BlockSpec(memory_space=pl.ANY)
    po, rotation = pl.pallas_call(
        functools.partial(exchange_kernel, split, n_sems),
        out_shape=(
            jax.ShapeDtypeStruct((GROUP, tier, chunk), bf16),
            jax.ShapeDtypeStruct((rows, parcels), f32),
        ),
        in_specs=[hbm, vmem, vmem, hbm],
        out_specs=(vmem,) * 2,
        scratch_shapes=[
            pltpu.VMEM((frames, gray), bf16),
            pltpu.VMEM((NC, parcels // NC, gray), bf16),
            pltpu.VMEM((NX, NZ, rows, frames), f32),
            pltpu.VMEM((NX, NZ, rows, frames), f32),
            pltpu.VMEM((NX, NZ, rows, frames), f32),
            pltpu.VMEM((NX - 1, NZ, rows, split), f32),
            pltpu.VMEM((NZ - 1, NX, rows, rest), f32),
            pltpu.VMEM((NZ, rows, split), f32),
            pltpu.VMEM((NX, rows, rest), f32),
            pltpu.VMEM((NZ - 1, rows, split), f32),
            pltpu.VMEM((NX - 1, rows, rest), f32),
            pltpu.VMEM((NX, 8, chunk), f32),
            pltpu.VMEM((NX, 8, chunk), f32),
            pltpu.VMEM((NX, 8, chunk), f32),
            pltpu.VMEM((NX - 1, 8, chunk), f32),
            pltpu.VMEM((8, chunk), f32),
            pltpu.VMEM((NZ - 1, 8, chunk), f32),
            pltpu.VMEM((GROUP, tier, frames), bf16),
            pltpu.VMEM((GROUP, tier, parcels), bf16),
            pltpu.VMEM((NZ, rows, frames), bf16),
            pltpu.VMEM((GROUP, tier, chunk), bf16),
            pltpu.VMEM((NPART, NZ, rows, width), f32),
            pltpu.VMEM((NPART, NZ - 1, rows, width), f32),
            pltpu.VMEM((8, 128), f32),
            pltpu.VMEM((NZ - 1, 8, 128), f32),
            pltpu.VMEM((8, 128), f32),
            pltpu.VMEM((NX - 1, 8, 128), f32),
            pltpu.VMEM((8, 128), f32),
            pltpu.VMEM((8, 128), f32),
            pltpu.VMEM((NPART, NX, NZ, NC, rows, width), bf16),
            pltpu.VMEM((NPART, rows, width), f32),
            pltpu.VMEM((parcels, parcels), f32),
            pltpu.VMEM((2, parcels, parcels), bf16),
            pltpu.VMEM((parcels, parcels), f32),
            pltpu.VMEM((parcels, parcels), bf16),
            pltpu.SemaphoreType.DMA((n_sems,)),
            pltpu.SemaphoreType.DMA((n_sems,)),
            pltpu.SemaphoreType.DMA((2,)),
        ],
        compiler_params=pltpu.CompilerParams(
            collective_id=0, has_side_effects=True, vmem_limit_bytes=56 * 2**20
        ),
        name="exchange",
    )(series, labels, tier_index, template)
    return pl.pallas_call(
        finish_kernel,
        out_shape=(
            jax.ShapeDtypeStruct((tier, parcels), bf16),
            jax.ShapeDtypeStruct((rows, parcels), f32),
        ),
        in_specs=[vmem] * 2,
        out_specs=(vmem,) * 2,
        name="finish",
    )(po, rotation)


def solution(mesh):
    placed = (P("subj", "vert"), P("vert"), P("vert"), P("vert", None))
    return jax.shard_map(
        local,
        mesh=mesh,
        in_specs=placed,
        out_specs=(P("vert", "subj"), P("vert", "subj")),
        check_vma=False,
    )
```

```python
import functools

import jax
import jax.numpy as jnp
import numpy as np
from jax import lax
from jax.experimental import pallas as pl
from jax.experimental.pallas import tpu as pltpu
from jax.sharding import PartitionSpec as P

NS_STEPS = 4
NX, NZ, NC = 4, 8, 2
PLANE = NX * NZ * NC
GROUP = NX * NC
MESH = pl.DeviceIdType.MESH
NPART = 2
NT = (((1,), (1,)), ((), ()))
NN = (((1,), (0,)), ((), ()))
CORE = (0, 0, 1)
XS = [(dx, 0, 0) for dx in range(1, NX)]
ZS = [(0, dz, 0) for dz in range(1, NZ)]
BESIDE = [(1, 0, 0), (NX - 1, 0, 0)]
DIAGONAL = [(dx, 0, 1) for dx in range(1, NX)]


def dot(a, b, dims):
    return lax.dot_general(a, b, dims, preferred_element_type=jnp.float32)


def standardize_rows(block):
    centered = block - jnp.mean(block, axis=1, keepdims=True)
    return centered / jnp.sqrt(jnp.mean(centered * centered, axis=1, keepdims=True) + 1e-05)


def exchange_kernel(
    late,
    split,
    n_sems,
    series_hbm,
    labels_ref,
    tier_ref,
    template_hbm,
    po,
    rotation_ref,
    series,
    onehot,
    part,
    part_in,
    mine,
    a_in,
    b_in,
    a_sum,
    b_sum,
    a_in2,
    b_in2,
    cnt_out,
    cnt_in,
    cnt_mine,
    cnt_xin,
    cnt_x,
    cnt_zin,
    vz,
    tm,
    pz,
    pg,
    cx,
    cx_in,
    norm_part,
    norm_zin,
    norm_z,
    norm_xin,
    norm_x,
    norm_cin,
    xg,
    own_rows,
    gram,
    gram16,
    step_sum,
    step16,
    send_sems,
    recv_sems,
    local_sems,
):
    frames, gray = series.shape
    rows = cx.shape[2]
    width = cx.shape[3]
    parcels = NPART * width
    chunk = NZ * rows
    tier = vz.shape[1]
    me = lax.axis_index("vert")
    c = lax.rem(me, NC)
    z = lax.rem(me // NC, NZ)
    x = me // (NC * NZ)
    member = x * NC + c

    def x_at(dx):
        return lax.rem(x + dx + NX, NX)

    def z_at(dz):
        return lax.rem(z + dz + NZ, NZ)

    def device(offset):
        dx, dz, dc = offset
        return {"vert": (x_at(dx) * NZ + z_at(dz)) * NC + lax.rem(c + dc, NC)}

    groups = []

    class Group:
        def __init__(self, sized):
            self.sized = sized
            self.k = len(groups)
            groups.append(self)

        def send(self, src, dst, offset):
            pltpu.make_async_remote_copy(
                src_ref=src,
                dst_ref=dst,
                send_sem=send_sems.at[self.k],
                recv_sem=recv_sems.at[self.k],
                device_id=device(offset),
                device_id_type=MESH,
            ).start()

        def wait(self, sems):
            pltpu.make_async_copy(self.sized, self.sized, sems.at[self.k]).wait()

        def wait_recv(self):
            self.wait(recv_sems)

    def exchange(src, dst, offset):
        group = Group(dst)
        group.send(src, dst, offset)
        return group

    def scatter(pick, dst, offsets):
        group = Group(dst)
        for k, offset in enumerate(offsets):
            group.send(pick(k + 1), dst.at[k], offset)
        return group

    def repeat(block, sized, offsets):
        group = Group(sized)
        for offset in offsets:
            group.send(block, block, offset)
        return group

    series_copy = pltpu.make_async_copy(series_hbm, series, local_sems.at[0])
    series_copy.start()
    template_copy = pltpu.make_async_copy(template_hbm, tm.at[member], local_sems.at[1])
    template_copy.start()

    barrier = pltpu.get_barrier_semaphore()
    peers = [CORE] + XS + DIAGONAL + ZS
    for offset in peers:
        pl.semaphore_signal(barrier, inc=1, device_id=device(offset), device_id_type=MESH)

    half = parcels // NC

    def fill_onehot(side, core):
        q = lax.broadcasted_iota(jnp.int32, (half, gray), 0)
        parcel = ((q // rows) * NC + core) * rows + q % rows
        onehot[side] = (parcel == labels_ref[...].reshape(1, gray)).astype(jnp.bfloat16)

    fill_onehot(0, 1 - c)
    template_copy.wait()
    pl.semaphore_wait(barrier, len(peers))
    tm_hop = repeat(tm.at[member], tm.at[0:2], BESIDE)
    series_copy.wait()
    spans = [(split, frames), (late, split), (0, late)]
    part[...] = dot(onehot[0], series[...], NT).reshape(part.shape)
    core_sends = [
        exchange(part.at[:, :, :, lo:hi], part_in.at[:, :, :, lo:hi], CORE) for lo, hi in spans
    ]
    fill_onehot(1, c)
    mine[...] = dot(onehot[1], series[...], NT).reshape(mine.shape)

    def add_core(n):
        lo, hi = spans[n]
        core_sends[n].wait_recv()
        mine[:, :, :, lo:hi] = mine[:, :, :, lo:hi] + part_in[:, :, :, lo:hi]

    def send_x(n):
        lo, hi = spans[n]
        near = Group(a_in.at[0:2, :, :, lo:hi])
        for dx in (1, NX - 1):
            near.send(mine.at[x_at(dx), :, :, lo:hi], a_in.at[dx - 1, :, :, lo:hi], (dx, 0, 0))
        far = exchange(mine.at[x_at(2), :, :, lo:hi], a_in.at[1, :, :, lo:hi], XS[1])
        return near, far

    def sum_x(n):
        lo, hi = spans[n]
        total = mine[x, :, :, lo:hi] + a_in[0, :, :, lo:hi]
        a_sum[:, :, lo:hi] = total + a_in[1, :, :, lo:hi] + a_in[2, :, :, lo:hi]
        group = Group(a_in2.at[:, :, lo:hi])
        for k, offset in enumerate(ZS):
            group.send(a_sum.at[z_at(k + 1), :, lo:hi], a_in2.at[k, :, lo:hi], offset)
        return group

    add_core(0)
    lo, hi = spans[0]
    b_group = scatter(lambda k: mine.at[:, z_at(k), :, lo:hi], b_in, ZS)
    add_core(1)
    a_near, a_far = send_x(1)
    add_core(2)
    a_near2, a_far2 = send_x(2)

    ones = jnp.ones((8, gray), jnp.bfloat16)
    away = dot(ones, onehot[0], NT)
    for k in range(NX):
        cnt_out[k] = away[:, k * chunk : (k + 1) * chunk]
    cnt_core = exchange(cnt_out, cnt_in, CORE)
    home = dot(ones, onehot[1], NT)

    ids = jnp.broadcast_to(tier_ref[...].reshape(1, tier).astype(jnp.float32), (tier, tier))
    diagonal = lax.broadcasted_iota(jnp.int32, (tier, tier), 0) == lax.broadcasted_iota(
        jnp.int32, (tier, tier), 1
    )
    column = jnp.sum(jnp.where(diagonal, ids, 0.0), axis=1, keepdims=True).astype(jnp.int32)
    pick = (column == lax.broadcasted_iota(jnp.int32, (tier, gray), 1)).astype(jnp.bfloat16)
    vz[member] = standardize_rows(dot(pick, series[...], NT)).astype(jnp.bfloat16)

    cnt_core.wait_recv()
    for k in range(NX):
        cnt_mine[k] = home[:, k * chunk : (k + 1) * chunk] + cnt_in[k]
    cnt_xs = scatter(lambda k: cnt_mine.at[x_at(k)], cnt_xin, XS)

    def to_core(held):
        group = Group(held.at[0:NX])
        group.send(held.at[member], held.at[member], CORE)
        return group

    tm_core, vz_core = to_core(tm), to_core(vz)

    left, right = x_at(-1) * NC + c, x_at(1) * NC + c
    opposite = x_at(2) * NC + c
    front, back = pl.ds(0, tier // 2), pl.ds(tier // 2, tier // 2)

    def second_hop(hop, held, core):
        hop.wait_recv()
        group = Group(held.at[0])
        for owner, piece, offset in ((left, front, BESIDE[0]), (right, back, BESIDE[1])):
            group.send(held.at[owner, piece], held.at[owner, piece], offset)
            core.send(held.at[owner], held.at[owner], CORE)
        return group

    def pass_opposite(hop, held, core):
        hop.wait_recv()
        core.send(held.at[opposite], held.at[opposite], CORE)

    a_near.wait_recv()
    a_far.wait_recv()
    a_group2 = sum_x(1)
    a_near2.wait_recv()
    vz_hop = repeat(vz.at[member], vz.at[0:2], BESIDE)
    a_far2.wait_recv()
    a_group3 = sum_x(2)
    b_group.wait_recv()
    total = mine[:, z, :, split:]
    for k in range(NZ - 1):
        total = total + b_in[k]
    b_sum[...] = total
    b_group2 = scatter(lambda k: b_sum.at[x_at(k)], b_in2, XS)
    cnt_xs.wait_recv()
    cnt_x[...] = cnt_mine[x] + cnt_xin[0] + cnt_xin[1] + cnt_xin[2]
    cnt_zs = scatter(lambda k: cnt_x, cnt_zin, ZS)
    vz_hop2 = second_hop(vz_hop, vz, vz_core)
    tm_hop2 = second_hop(tm_hop, tm, tm_core)

    for group in (b_group2, cnt_zs, a_group2, a_group3):
        group.wait_recv()
    a_total = a_sum[z]
    for k in range(NZ - 1):
        a_total = a_total + a_in2[k]
    b_total = b_sum[x] + b_in2[0] + b_in2[1] + b_in2[2]
    counts = cnt_x[...]
    for k in range(NZ - 1):
        counts = counts + cnt_zin[k]
    spot = lax.broadcasted_iota(jnp.int32, (rows, chunk), 1) == z * rows + lax.broadcasted_iota(
        jnp.int32, (rows, chunk), 0
    )
    counts = jnp.concatenate([counts] * (rows // 8), axis=0)
    count = jnp.sum(jnp.where(spot, counts, 0.0), axis=1, keepdims=True)
    sums = jnp.concatenate([a_total, b_total], axis=1)
    pz[z] = standardize_rows(sums / jnp.maximum(count, 1.0)).astype(jnp.bfloat16)
    pz_group = repeat(pz.at[z], pz.at[0 : NZ - 1], ZS)
    pass_opposite(vz_hop2, vz, vz_core)
    pass_opposite(tm_hop2, tm, tm_core)
    for group in (vz_core, pz_group):
        group.wait_recv()

    scale = np.float32(1.0 / np.sqrt(frames))
    pzs = pz[...].reshape(chunk, frames)
    vzs = vz[...].reshape(GROUP * tier, frames)
    turned = (dot(pzs, vzs, NT) * scale).astype(jnp.bfloat16)
    tm_core.wait_recv()

    near_z, far_z = [1, NZ - 1, 2, NZ - 2], [3, NZ - 3, 4]

    def scatter_cross(n):
        both = []
        for distances in (far_z, near_z):
            group = Group(cx_in.at[n, 0 : len(distances)])
            for dz in distances:
                group.send(cx.at[n, z_at(dz)], cx_in.at[n, dz - 1], ZS[dz - 1])
            both.append(group)
        return both

    def cross_part(n):
        columns = tm[:, :, n * width : (n + 1) * width].reshape(GROUP * tier, width)
        cx[n] = dot(turned, columns, NN).reshape(NZ, rows, width)

    cross_part(0)
    cx_groups = [scatter_cross(0)]
    for n in range(1, NPART):
        cross_part(n)
        cx_groups.append(scatter_cross(n))

    pg[...] = (dot(vzs, pzs, NT) * scale).astype(jnp.bfloat16).reshape(GROUP, tier, chunk)
    po[member] = pg[member]
    po_group = Group(po.at[0 : GROUP - 1])
    for dx, _, dc in [CORE] + XS + DIAGONAL:
        owner = x_at(dx) * NC + lax.rem(c + dc, NC)
        po_group.send(pg.at[owner], po.at[member], (dx, 0, dc))

    near_first = range(1, NZ // 2 + 1)
    xg_z, xg_x = [], [[] for _ in range(NPART)]
    xg_c = [Group(xg.at[n, :, :, 0]) for n in range(NPART)]

    def forward(n, at_z):
        block = xg.at[n, x, at_z, c]
        xg_x[n].append((at_z, repeat(block, xg.at[n, 0 : NX - 1, 0, 0], XS)))

    def own_part(n):
        far, near = cx_groups[n]
        near.wait_recv()
        far.wait_recv()
        cross = cx[n, z]
        for k in range(NZ - 1):
            cross = cross + cx_in[n, k]
        own_rows[n] = cross
        xg[n, x, z, c] = cross.astype(jnp.bfloat16)
        block = xg.at[n, x, z, c]
        by_distance = []
        for dz in near_first:
            pair = [dz] if 2 * dz == NZ else [dz, NZ - dz]
            by_distance.append(
                (pair, repeat(block, xg.at[n, 0, 0 : len(pair), 0], [ZS[k - 1] for k in pair]))
            )
        xg_z.append(by_distance)
        forward(n, z)
        return jnp.sum(jnp.sum(cross * cross, axis=1, keepdims=True), axis=0, keepdims=True)

    def forward_z(n, distances):
        for pair, group in xg_z[n][distances]:
            group.wait_recv()
            for dz in pair:
                forward(n, z_at(-dz))

    first_cross = groups.index(cx_groups[0][0])
    for group in groups[:first_cross]:
        group.wait(send_sems)
    square = own_part(0)
    for n in range(1, NPART):
        forward_z(n - 1, slice(0, 2))
        square = square + own_part(n)
        if n == NPART - 1:
            norm_part[...] = jnp.broadcast_to(square, norm_part.shape)
            norm_zs = scatter(lambda k: norm_part, norm_zin, ZS)
        forward_z(n - 1, slice(2, None))
    forward_z(NPART - 1, slice(0, None))
    norm_zs.wait_recv()
    norm = norm_part[...]
    for k in range(NZ - 1):
        norm = norm + norm_zin[k]
    norm_z[...] = norm
    norm_xs = scatter(lambda k: norm_z, norm_xin, XS)

    def pass_core(n, blocks):
        for at_z, group in blocks:
            group.wait_recv()
            blocks_in = xg.at[n, :, at_z, c]
            xg_c[n].send(blocks_in, blocks_in, CORE)

    square_block = parcels // 4
    edges = [(lo, lo + square_block) for lo in range(0, parcels, square_block)]

    def add_gram(n, lo, hi):
        rows_n = xg[n].reshape(parcels, width)
        piece = dot(rows_n[lo:], rows_n[lo:hi], NT)
        gram[lo:, lo:hi] = piece if n == 0 else gram[lo:, lo:hi] + piece

    for n in range(NPART):
        if n == 0:
            pass_core(0, xg_x[0])
        xg_c[n].wait_recv()
        for k, (lo, hi) in enumerate(edges):
            add_gram(n, lo, hi)
            if n + 1 < NPART:
                pass_core(n + 1, xg_x[n + 1][2 * k : 2 * k + 2])
            if n + 1 == NPART - 1 and k == 1:
                norm_xs.wait_recv()
                norm_x[...] = norm_z[...] + norm_xin[0] + norm_xin[1] + norm_xin[2]
                norm_core = exchange(norm_x, norm_cin, CORE)
    norm_core.wait_recv()
    total = norm_x[...] + norm_cin[...]
    unit = 1.0 / jnp.sqrt(total[0:1, 0:1] + 1e-06)

    def mirror(held, lo, hi, values):
        held[lo:, lo:hi] = values.astype(jnp.bfloat16)
        if hi < parcels:
            held[lo:hi, hi:] = values[hi - lo :].T.astype(jnp.bfloat16)

    def next_gram(old, new):
        for lo, hi in edges:
            values = 1.5 * gram[lo:, lo:hi] - 0.5 * dot(old[lo:, :], old[:, lo:hi], NN)
            step_sum[lo:, lo:hi] = values
            mirror(step16, lo, hi, values)
        for lo, hi in edges:
            values = 1.5 * step_sum[lo:, lo:hi] - 0.5 * dot(step16[lo:, :], old[:, lo:hi], NN)
            gram[lo:, lo:hi] = values
            mirror(new, lo, hi, values)

    def thin(values, matrix):
        high = values.astype(jnp.bfloat16)
        low = (values - high.astype(jnp.float32)).astype(jnp.bfloat16)
        product = dot(jnp.concatenate([high, low], axis=0), matrix, NN)
        return product[:rows] + product[rows:]

    def step_rows(values, held):
        return 1.5 * values - 0.5 * thin(values, held[...])

    for lo, hi in edges:
        values = gram[lo:, lo:hi] * (unit * unit)
        gram[lo:, lo:hi] = values
        mirror(gram16.at[0], lo, hi, values)
    identity = (
        lax.broadcasted_iota(jnp.int32, (rows, parcels), 1)
        == me * rows + lax.broadcasted_iota(jnp.int32, (rows, parcels), 0)
    ).astype(jnp.float32)
    for step in range(NS_STEPS - 1):
        held = gram16.at[step % 2]
        if step == 0:
            own = held[pl.ds(pl.multiple_of(me * rows, rows), rows), :]
            factor = 1.5 * identity - 0.5 * own.astype(jnp.float32)
        else:
            factor = step_rows(factor, held)
        if step < NS_STEPS - 2:
            next_gram(held, gram16.at[(step + 1) % 2])
    product = step_rows(step_rows(thin(factor, held[...]), held), held)
    factor = 1.5 * factor - 0.5 * product
    linear = np.float32(1.5**NS_STEPS)
    rest = factor - linear * identity
    for n in range(NPART):
        out = linear * own_rows[n] + thin(rest, xg[n].reshape(parcels, width))
        rotation_ref[:, n * width : (n + 1) * width] = out * unit * jnp.sqrt(jnp.float32(parcels))
    po_group.wait_recv()
    for group in groups[first_cross:]:
        group.wait(send_sems)
    assert len(groups) == n_sems, len(groups)


def finish_kernel(po_ref, rows_ref, profiles_ref, rotation_ref):
    chunk = po_ref.shape[2]
    rows = rows_ref.shape[0]
    rotation_ref[...] = rows_ref[...]
    wide = NC * chunk
    old = lax.broadcasted_iota(jnp.int32, (wide, wide), 0)
    new = lax.broadcasted_iota(jnp.int32, (wide, wide), 1)
    target = (((old % chunk) // rows) * NC + old // chunk) * rows + old % rows
    order = (target == new).astype(jnp.bfloat16)
    for k in range(NX):
        pair = jnp.concatenate([po_ref[NC * k + n] for n in range(NC)], axis=1)
        profiles_ref[:, k * wide : (k + 1) * wide] = dot(pair, order, NN).astype(jnp.bfloat16)


def local(series, labels, tier_index, template):
    frames, gray = series.shape
    tier, parcels = template.shape
    rows = parcels // PLANE
    chunk = NZ * rows
    width = parcels // NPART
    split = frames // 8 * 5 // 128 * 128
    late = split // 5 * 2 // 128 * 128
    rest = frames - split
    f32, bf16 = jnp.float32, jnp.bfloat16
    n_sems = 55
    vmem = pl.BlockSpec(memory_space=pltpu.VMEM)
    hbm = pl.BlockSpec(memory_space=pl.ANY)
    po, rotation = pl.pallas_call(
        functools.partial(exchange_kernel, late, split, n_sems),
        out_shape=(
            jax.ShapeDtypeStruct((GROUP, tier, chunk), bf16),
            jax.ShapeDtypeStruct((rows, parcels), f32),
        ),
        in_specs=[hbm, vmem, vmem, hbm],
        out_specs=(vmem,) * 2,
        scratch_shapes=[
            pltpu.VMEM((frames, gray), bf16),
            pltpu.VMEM((NC, parcels // NC, gray), bf16),
            pltpu.VMEM((NX, NZ, rows, frames), f32),
            pltpu.VMEM((NX, NZ, rows, frames), f32),
            pltpu.VMEM((NX, NZ, rows, frames), f32),
            pltpu.VMEM((NX - 1, NZ, rows, split), f32),
            pltpu.VMEM((NZ - 1, NX, rows, rest), f32),
            pltpu.VMEM((NZ, rows, split), f32),
            pltpu.VMEM((NX, rows, rest), f32),
            pltpu.VMEM((NZ - 1, rows, split), f32),
            pltpu.VMEM((NX - 1, rows, rest), f32),
            pltpu.VMEM((NX, 8, chunk), f32),
            pltpu.VMEM((NX, 8, chunk), f32),
            pltpu.VMEM((NX, 8, chunk), f32),
            pltpu.VMEM((NX - 1, 8, chunk), f32),
            pltpu.VMEM((8, chunk), f32),
            pltpu.VMEM((NZ - 1, 8, chunk), f32),
            pltpu.VMEM((GROUP, tier, frames), bf16),
            pltpu.VMEM((GROUP, tier, parcels), bf16),
            pltpu.VMEM((NZ, rows, frames), bf16),
            pltpu.VMEM((GROUP, tier, chunk), bf16),
            pltpu.VMEM((NPART, NZ, rows, width), f32),
            pltpu.VMEM((NPART, NZ - 1, rows, width), f32),
            pltpu.VMEM((8, 128), f32),
            pltpu.VMEM((NZ - 1, 8, 128), f32),
            pltpu.VMEM((8, 128), f32),
            pltpu.VMEM((NX - 1, 8, 128), f32),
            pltpu.VMEM((8, 128), f32),
            pltpu.VMEM((8, 128), f32),
            pltpu.VMEM((NPART, NX, NZ, NC, rows, width), bf16),
            pltpu.VMEM((NPART, rows, width), f32),
            pltpu.VMEM((parcels, parcels), f32),
            pltpu.VMEM((2, parcels, parcels), bf16),
            pltpu.VMEM((parcels, parcels), f32),
            pltpu.VMEM((parcels, parcels), bf16),
            pltpu.SemaphoreType.DMA((n_sems,)),
            pltpu.SemaphoreType.DMA((n_sems,)),
            pltpu.SemaphoreType.DMA((2,)),
        ],
        compiler_params=pltpu.CompilerParams(
            collective_id=0, has_side_effects=True, vmem_limit_bytes=56 * 2**20
        ),
        name="exchange",
    )(series, labels, tier_index, template)
    return pl.pallas_call(
        finish_kernel,
        out_shape=(
            jax.ShapeDtypeStruct((tier, parcels), bf16),
            jax.ShapeDtypeStruct((rows, parcels), f32),
        ),
        in_specs=[vmem] * 2,
        out_specs=(vmem,) * 2,
        name="finish",
    )(po, rotation)


def solution(mesh):
    placed = (P("subj", "vert"), P("vert"), P("vert"), P("vert", None))
    return jax.shard_map(
        local,
        mesh=mesh,
        in_specs=placed,
        out_specs=(P("vert", "subj"), P("vert", "subj")),
        check_vma=False,
    )
```

```python
import functools

import jax
import jax.numpy as jnp
import numpy as np
from jax import lax
from jax.experimental import pallas as pl
from jax.experimental.pallas import tpu as pltpu
from jax.sharding import PartitionSpec as P

NS_STEPS = 4
NX, NZ, NC = 4, 8, 2
PLANE = NX * NZ * NC
GROUP = NX * NC
MESH = pl.DeviceIdType.MESH
NPART = 2
NT = (((1,), (1,)), ((), ()))
NN = (((1,), (0,)), ((), ()))
CORE = (0, 0, 1)
XS = [(dx, 0, 0) for dx in range(1, NX)]
ZS = [(0, dz, 0) for dz in range(1, NZ)]
BESIDE = [(1, 0, 0), (NX - 1, 0, 0)]
DIAGONAL = [(dx, 0, 1) for dx in range(1, NX)]


def dot(a, b, dims):
    return lax.dot_general(a, b, dims, preferred_element_type=jnp.float32)


def standardize_rows(block):
    centered = block - jnp.mean(block, axis=1, keepdims=True)
    return centered / jnp.sqrt(jnp.mean(centered * centered, axis=1, keepdims=True) + 1e-05)


def exchange_kernel(
    late,
    split,
    n_sems,
    series_hbm,
    labels_ref,
    tier_ref,
    template_hbm,
    po,
    rotation_ref,
    series,
    onehot,
    part,
    part_in,
    mine,
    a_in,
    b_in,
    a_sum,
    b_sum,
    a_in2,
    b_in2,
    cnt_out,
    cnt_in,
    cnt_mine,
    cnt_xin,
    cnt_x,
    cnt_zin,
    vz,
    tm,
    pz,
    pg,
    cx,
    cx_in,
    norm_part,
    norm_zin,
    norm_z,
    norm_xin,
    norm_x,
    norm_cin,
    xg,
    own_rows,
    gram,
    gram16,
    step_sum,
    step16,
    send_sems,
    recv_sems,
    local_sems,
):
    frames, gray = series.shape
    rows = cx.shape[2]
    width = cx.shape[3]
    parcels = NPART * width
    chunk = NZ * rows
    tier = vz.shape[1]
    me = lax.axis_index("vert")
    c = lax.rem(me, NC)
    z = lax.rem(me // NC, NZ)
    x = me // (NC * NZ)
    member = x * NC + c

    def x_at(dx):
        return lax.rem(x + dx + NX, NX)

    def z_at(dz):
        return lax.rem(z + dz + NZ, NZ)

    def device(offset):
        dx, dz, dc = offset
        return {"vert": (x_at(dx) * NZ + z_at(dz)) * NC + lax.rem(c + dc, NC)}

    groups = []

    class Group:
        def __init__(self, sized):
            self.sized = sized
            self.k = len(groups)
            groups.append(self)

        def send(self, src, dst, offset):
            pltpu.make_async_remote_copy(
                src_ref=src,
                dst_ref=dst,
                send_sem=send_sems.at[self.k],
                recv_sem=recv_sems.at[self.k],
                device_id=device(offset),
                device_id_type=MESH,
            ).start()

        def wait(self, sems):
            pltpu.make_async_copy(self.sized, self.sized, sems.at[self.k]).wait()

        def wait_recv(self):
            self.wait(recv_sems)

    def exchange(src, dst, offset):
        group = Group(dst)
        group.send(src, dst, offset)
        return group

    def scatter(pick, dst, offsets):
        group = Group(dst)
        for k, offset in enumerate(offsets):
            group.send(pick(k + 1), dst.at[k], offset)
        return group

    def repeat(block, sized, offsets):
        group = Group(sized)
        for offset in offsets:
            group.send(block, block, offset)
        return group

    barrier = pltpu.get_barrier_semaphore()
    peers = [CORE] + XS + DIAGONAL + ZS
    for offset in peers:
        pl.semaphore_signal(barrier, inc=1, device_id=device(offset), device_id_type=MESH)
    template_copy = pltpu.make_async_copy(template_hbm, tm.at[member], local_sems.at[1])
    template_copy.start()
    series_copy = pltpu.make_async_copy(series_hbm, series, local_sems.at[0])
    series_copy.start()

    half = parcels // NC

    def fill_onehot(side, core):
        q = lax.broadcasted_iota(jnp.int32, (half, gray), 0)
        parcel = ((q // rows) * NC + core) * rows + q % rows
        onehot[side] = (parcel == labels_ref[...].reshape(1, gray)).astype(jnp.bfloat16)

    fill_onehot(0, 1 - c)
    template_copy.wait()
    pl.semaphore_wait(barrier, len(peers))
    tm_hop = repeat(tm.at[member], tm.at[0:2], BESIDE)
    series_copy.wait()
    spans = [(split, frames), (late, split), (0, late)]
    part[...] = dot(onehot[0], series[...], NT).reshape(part.shape)
    core_sends = [
        exchange(part.at[:, :, :, lo:hi], part_in.at[:, :, :, lo:hi], CORE) for lo, hi in spans
    ]
    fill_onehot(1, c)
    mine[...] = dot(onehot[1], series[...], NT).reshape(mine.shape)

    def add_core(n):
        lo, hi = spans[n]
        core_sends[n].wait_recv()
        mine[:, :, :, lo:hi] = mine[:, :, :, lo:hi] + part_in[:, :, :, lo:hi]

    def send_x(n):
        lo, hi = spans[n]
        near = Group(a_in.at[0:2, :, :, lo:hi])
        for dx in (1, NX - 1):
            near.send(mine.at[x_at(dx), :, :, lo:hi], a_in.at[dx - 1, :, :, lo:hi], (dx, 0, 0))
        far = exchange(mine.at[x_at(2), :, :, lo:hi], a_in.at[1, :, :, lo:hi], XS[1])
        return near, far

    def sum_x(n):
        lo, hi = spans[n]
        total = mine[x, :, :, lo:hi] + a_in[0, :, :, lo:hi]
        a_sum[:, :, lo:hi] = total + a_in[1, :, :, lo:hi] + a_in[2, :, :, lo:hi]
        group = Group(a_in2.at[:, :, lo:hi])
        for k, offset in enumerate(ZS):
            group.send(a_sum.at[z_at(k + 1), :, lo:hi], a_in2.at[k, :, lo:hi], offset)
        return group

    add_core(0)
    lo, hi = spans[0]
    b_group = scatter(lambda k: mine.at[:, z_at(k), :, lo:hi], b_in, ZS)
    add_core(1)
    a_near, a_far = send_x(1)
    add_core(2)
    a_near2, a_far2 = send_x(2)

    ones = jnp.ones((8, gray), jnp.bfloat16)
    away = dot(ones, onehot[0], NT)
    for k in range(NX):
        cnt_out[k] = away[:, k * chunk : (k + 1) * chunk]
    cnt_core = exchange(cnt_out, cnt_in, CORE)
    home = dot(ones, onehot[1], NT)

    ids = jnp.broadcast_to(tier_ref[...].reshape(1, tier).astype(jnp.float32), (tier, tier))
    diagonal = lax.broadcasted_iota(jnp.int32, (tier, tier), 0) == lax.broadcasted_iota(
        jnp.int32, (tier, tier), 1
    )
    column = jnp.sum(jnp.where(diagonal, ids, 0.0), axis=1, keepdims=True).astype(jnp.int32)
    pick = (column == lax.broadcasted_iota(jnp.int32, (tier, gray), 1)).astype(jnp.bfloat16)
    vz[member] = standardize_rows(dot(pick, series[...], NT)).astype(jnp.bfloat16)

    cnt_core.wait_recv()
    for k in range(NX):
        cnt_mine[k] = home[:, k * chunk : (k + 1) * chunk] + cnt_in[k]
    cnt_xs = scatter(lambda k: cnt_mine.at[x_at(k)], cnt_xin, XS)

    def to_core(held):
        group = Group(held.at[0:NX])
        group.send(held.at[member], held.at[member], CORE)
        return group

    tm_core, vz_core = to_core(tm), to_core(vz)

    left, right = x_at(-1) * NC + c, x_at(1) * NC + c
    opposite = x_at(2) * NC + c
    front, back = pl.ds(0, tier // 2), pl.ds(tier // 2, tier // 2)

    def second_hop(hop, held, core):
        hop.wait_recv()
        group = Group(held.at[0])
        for owner, piece, offset in ((left, front, BESIDE[0]), (right, back, BESIDE[1])):
            group.send(held.at[owner, piece], held.at[owner, piece], offset)
            core.send(held.at[owner], held.at[owner], CORE)
        return group

    def pass_opposite(hop, held, core):
        hop.wait_recv()
        core.send(held.at[opposite], held.at[opposite], CORE)

    a_near.wait_recv()
    vz_hop = repeat(vz.at[member], vz.at[0:2], BESIDE)
    a_far.wait_recv()
    a_group2 = sum_x(1)
    a_near2.wait_recv()
    a_far2.wait_recv()
    a_group3 = sum_x(2)
    b_group.wait_recv()
    total = mine[:, z, :, split:]
    for k in range(NZ - 1):
        total = total + b_in[k]
    b_sum[...] = total
    b_group2 = scatter(lambda k: b_sum.at[x_at(k)], b_in2, XS)
    cnt_xs.wait_recv()
    cnt_x[...] = cnt_mine[x] + cnt_xin[0] + cnt_xin[1] + cnt_xin[2]
    cnt_zs = scatter(lambda k: cnt_x, cnt_zin, ZS)
    vz_hop2 = second_hop(vz_hop, vz, vz_core)
    tm_hop2 = second_hop(tm_hop, tm, tm_core)

    for group in (b_group2, cnt_zs, a_group2, a_group3):
        group.wait_recv()
    a_total = a_sum[z]
    for k in range(NZ - 1):
        a_total = a_total + a_in2[k]
    b_total = b_sum[x] + b_in2[0] + b_in2[1] + b_in2[2]
    counts = cnt_x[...]
    for k in range(NZ - 1):
        counts = counts + cnt_zin[k]
    spot = lax.broadcasted_iota(jnp.int32, (rows, chunk), 1) == z * rows + lax.broadcasted_iota(
        jnp.int32, (rows, chunk), 0
    )
    counts = jnp.concatenate([counts] * (rows // 8), axis=0)
    count = jnp.sum(jnp.where(spot, counts, 0.0), axis=1, keepdims=True)
    sums = jnp.concatenate([a_total, b_total], axis=1)
    pz[z] = standardize_rows(sums / jnp.maximum(count, 1.0)).astype(jnp.bfloat16)
    pz_group = repeat(pz.at[z], pz.at[0 : NZ - 1], ZS)
    pass_opposite(vz_hop2, vz, vz_core)
    pass_opposite(tm_hop2, tm, tm_core)
    for group in (vz_core, pz_group):
        group.wait_recv()

    scale = np.float32(1.0 / np.sqrt(frames))
    pzs = pz[...].reshape(chunk, frames)
    vzs = vz[...].reshape(GROUP * tier, frames)
    turned = (dot(pzs, vzs, NT) * scale).astype(jnp.bfloat16)
    tm_core.wait_recv()

    near_z, far_z = [1, NZ - 1, 2, NZ - 2], [3, NZ - 3, 4]

    def scatter_cross(n):
        both = []
        for distances in (far_z, near_z):
            group = Group(cx_in.at[n, 0 : len(distances)])
            for dz in distances:
                group.send(cx.at[n, z_at(dz)], cx_in.at[n, dz - 1], ZS[dz - 1])
            both.append(group)
        return both

    def cross_part(n):
        columns = tm[:, :, n * width : (n + 1) * width].reshape(GROUP * tier, width)
        cx[n] = dot(turned, columns, NN).reshape(NZ, rows, width)

    cross_part(0)
    cx_groups = [scatter_cross(0)]
    for n in range(1, NPART):
        cross_part(n)
        cx_groups.append(scatter_cross(n))

    pg[...] = (dot(vzs, pzs, NT) * scale).astype(jnp.bfloat16).reshape(GROUP, tier, chunk)
    po[member] = pg[member]
    po_group = Group(po.at[0 : GROUP - 1])
    for dx, _, dc in [CORE] + XS + DIAGONAL:
        owner = x_at(dx) * NC + lax.rem(c + dc, NC)
        po_group.send(pg.at[owner], po.at[member], (dx, 0, dc))

    near_first = range(1, NZ // 2 + 1)
    xg_z, xg_x = [], [[] for _ in range(NPART)]
    xg_c = [Group(xg.at[n, :, :, 0]) for n in range(NPART)]

    def forward(n, at_z):
        block = xg.at[n, x, at_z, c]
        xg_x[n].append((at_z, repeat(block, xg.at[n, 0 : NX - 1, 0, 0], [XS[1], XS[0], XS[2]])))

    def own_part(n):
        far, near = cx_groups[n]
        near.wait_recv()
        far.wait_recv()
        cross = cx[n, z]
        for k in range(NZ - 1):
            cross = cross + cx_in[n, k]
        own_rows[n] = cross
        xg[n, x, z, c] = cross.astype(jnp.bfloat16)
        block = xg.at[n, x, z, c]
        by_distance = []
        for dz in near_first:
            pair = [dz] if 2 * dz == NZ else [dz, NZ - dz]
            by_distance.append(
                (pair, repeat(block, xg.at[n, 0, 0 : len(pair), 0], [ZS[k - 1] for k in pair]))
            )
        xg_z.append(by_distance)
        forward(n, z)
        return jnp.sum(jnp.sum(cross * cross, axis=1, keepdims=True), axis=0, keepdims=True)

    def forward_z(n, distances):
        for pair, group in xg_z[n][distances]:
            group.wait_recv()
            for dz in pair:
                forward(n, z_at(-dz))

    first_cross = groups.index(cx_groups[0][0])
    for group in groups[:first_cross]:
        group.wait(send_sems)
    square = own_part(0)
    for n in range(1, NPART):
        forward_z(n - 1, slice(0, 2))
        square = square + own_part(n)
        if n == NPART - 1:
            norm_part[...] = jnp.broadcast_to(square, norm_part.shape)
            norm_zs = scatter(lambda k: norm_part, norm_zin, ZS)
        forward_z(n - 1, slice(2, None))
    forward_z(NPART - 1, slice(0, None))
    norm_zs.wait_recv()
    norm = norm_part[...]
    for k in range(NZ - 1):
        norm = norm + norm_zin[k]
    norm_z[...] = norm
    norm_xs = scatter(lambda k: norm_z, norm_xin, XS)

    def pass_core(n, blocks):
        for at_z, group in blocks:
            group.wait_recv()
            blocks_in = xg.at[n, :, at_z, c]
            xg_c[n].send(blocks_in, blocks_in, CORE)

    square_block = parcels // 4
    edges = [(lo, lo + square_block) for lo in range(0, parcels, square_block)]

    def add_gram(n, lo, hi):
        rows_n = xg[n].reshape(parcels, width)
        piece = dot(rows_n[lo:], rows_n[lo:hi], NT)
        gram[lo:, lo:hi] = piece if n == 0 else gram[lo:, lo:hi] + piece

    for n in range(NPART):
        if n == 0:
            pass_core(0, xg_x[0])
        xg_c[n].wait_recv()
        for k, (lo, hi) in enumerate(edges):
            add_gram(n, lo, hi)
            if n + 1 < NPART:
                pass_core(n + 1, xg_x[n + 1][2 * k : 2 * k + 2])
            if n + 1 == NPART - 1 and k == 1:
                norm_xs.wait_recv()
                norm_x[...] = norm_z[...] + norm_xin[0] + norm_xin[1] + norm_xin[2]
                norm_core = exchange(norm_x, norm_cin, CORE)
    norm_core.wait_recv()
    total = norm_x[...] + norm_cin[...]
    unit = 1.0 / jnp.sqrt(total[0:1, 0:1] + 1e-06)

    def mirror(held, lo, hi, values):
        held[lo:, lo:hi] = values
        if hi < parcels:
            held[lo:hi, hi:] = values[hi - lo :].T

    def next_gram(old, new):
        for lo, hi in edges:
            values = 1.5 * gram[lo:, lo:hi] - 0.5 * dot(old[lo:, :], old[:, lo:hi], NN)
            step_sum[lo:, lo:hi] = values
            mirror(step16, lo, hi, values.astype(jnp.bfloat16))
        for lo, hi in edges:
            values = 1.5 * step_sum[lo:, lo:hi] - 0.5 * dot(step16[lo:, :], old[:, lo:hi], NN)
            gram[lo:, lo:hi] = values
            values = values.astype(jnp.bfloat16)
            mirror(new, lo, hi, values)

    def thin(values, matrix):
        high = values.astype(jnp.bfloat16)
        low = (values - high.astype(jnp.float32)).astype(jnp.bfloat16)
        product = dot(jnp.concatenate([high, low], axis=0), matrix, NN)
        return product[:rows] + product[rows:]

    def step_rows(values, held):
        return 1.5 * values - 0.5 * thin(values, held[...])

    for lo, hi in edges:
        values = gram[lo:, lo:hi] * (unit * unit)
        gram[lo:, lo:hi] = values
        mirror(gram16.at[0], lo, hi, values.astype(jnp.bfloat16))
    identity = (
        lax.broadcasted_iota(jnp.int32, (rows, parcels), 1)
        == me * rows + lax.broadcasted_iota(jnp.int32, (rows, parcels), 0)
    ).astype(jnp.float32)
    for step in range(NS_STEPS - 1):
        held = gram16.at[step % 2]
        if step == 0:
            own = held[pl.ds(pl.multiple_of(me * rows, rows), rows), :]
            factor = 1.5 * identity - 0.5 * own.astype(jnp.float32)
        else:
            factor = step_rows(factor, held)
        if step < NS_STEPS - 2:
            next_gram(held, gram16.at[(step + 1) % 2])
    product = step_rows(step_rows(thin(factor, held[...]), held), held)
    factor = 1.5 * factor - 0.5 * product
    linear = np.float32(1.5**NS_STEPS)
    rest = factor - linear * identity
    for n in range(NPART):
        out = linear * own_rows[n] + thin(rest, xg[n].reshape(parcels, width))
        rotation_ref[:, n * width : (n + 1) * width] = out * unit * jnp.sqrt(jnp.float32(parcels))
    po_group.wait_recv()
    for group in groups[first_cross:]:
        group.wait(send_sems)
    assert len(groups) == n_sems, len(groups)


def finish_kernel(po_ref, rows_ref, profiles_ref, rotation_ref):
    chunk = po_ref.shape[2]
    rows = rows_ref.shape[0]
    rotation_ref[...] = rows_ref[...]
    wide = NC * chunk
    old = lax.broadcasted_iota(jnp.int32, (wide, wide), 0)
    new = lax.broadcasted_iota(jnp.int32, (wide, wide), 1)
    target = (((old % chunk) // rows) * NC + old // chunk) * rows + old % rows
    order = (target == new).astype(jnp.bfloat16)
    for k in range(NX):
        pair = jnp.concatenate([po_ref[NC * k + n] for n in range(NC)], axis=1)
        profiles_ref[:, k * wide : (k + 1) * wide] = dot(pair, order, NN).astype(jnp.bfloat16)


def local(series, labels, tier_index, template):
    frames, gray = series.shape
    tier, parcels = template.shape
    rows = parcels // PLANE
    chunk = NZ * rows
    width = parcels // NPART
    split = frames // 8 * 5 // 128 * 128
    late = split // 5 * 2 // 128 * 128
    rest = frames - split
    f32, bf16 = jnp.float32, jnp.bfloat16
    n_sems = 55
    vmem = pl.BlockSpec(memory_space=pltpu.VMEM)
    hbm = pl.BlockSpec(memory_space=pl.ANY)
    po, rotation = pl.pallas_call(
        functools.partial(exchange_kernel, late, split, n_sems),
        out_shape=(
            jax.ShapeDtypeStruct((GROUP, tier, chunk), bf16),
            jax.ShapeDtypeStruct((rows, parcels), f32),
        ),
        in_specs=[hbm, vmem, vmem, hbm],
        out_specs=(vmem,) * 2,
        scratch_shapes=[
            pltpu.VMEM((frames, gray), bf16),
            pltpu.VMEM((NC, parcels // NC, gray), bf16),
            pltpu.VMEM((NX, NZ, rows, frames), f32),
            pltpu.VMEM((NX, NZ, rows, frames), f32),
            pltpu.VMEM((NX, NZ, rows, frames), f32),
            pltpu.VMEM((NX - 1, NZ, rows, split), f32),
            pltpu.VMEM((NZ - 1, NX, rows, rest), f32),
            pltpu.VMEM((NZ, rows, split), f32),
            pltpu.VMEM((NX, rows, rest), f32),
            pltpu.VMEM((NZ - 1, rows, split), f32),
            pltpu.VMEM((NX - 1, rows, rest), f32),
            pltpu.VMEM((NX, 8, chunk), f32),
            pltpu.VMEM((NX, 8, chunk), f32),
            pltpu.VMEM((NX, 8, chunk), f32),
            pltpu.VMEM((NX - 1, 8, chunk), f32),
            pltpu.VMEM((8, chunk), f32),
            pltpu.VMEM((NZ - 1, 8, chunk), f32),
            pltpu.VMEM((GROUP, tier, frames), bf16),
            pltpu.VMEM((GROUP, tier, parcels), bf16),
            pltpu.VMEM((NZ, rows, frames), bf16),
            pltpu.VMEM((GROUP, tier, chunk), bf16),
            pltpu.VMEM((NPART, NZ, rows, width), f32),
            pltpu.VMEM((NPART, NZ - 1, rows, width), f32),
            pltpu.VMEM((8, 128), f32),
            pltpu.VMEM((NZ - 1, 8, 128), f32),
            pltpu.VMEM((8, 128), f32),
            pltpu.VMEM((NX - 1, 8, 128), f32),
            pltpu.VMEM((8, 128), f32),
            pltpu.VMEM((8, 128), f32),
            pltpu.VMEM((NPART, NX, NZ, NC, rows, width), bf16),
            pltpu.VMEM((NPART, rows, width), f32),
            pltpu.VMEM((parcels, parcels), f32),
            pltpu.VMEM((2, parcels, parcels), bf16),
            pltpu.VMEM((parcels, parcels), f32),
            pltpu.VMEM((parcels, parcels), bf16),
            pltpu.SemaphoreType.DMA((n_sems,)),
            pltpu.SemaphoreType.DMA((n_sems,)),
            pltpu.SemaphoreType.DMA((2,)),
        ],
        compiler_params=pltpu.CompilerParams(
            collective_id=0, has_side_effects=True, vmem_limit_bytes=56 * 2**20
        ),
        name="exchange",
    )(series, labels, tier_index, template)
    return pl.pallas_call(
        finish_kernel,
        out_shape=(
            jax.ShapeDtypeStruct((tier, parcels), bf16),
            jax.ShapeDtypeStruct((rows, parcels), f32),
        ),
        in_specs=[vmem] * 2,
        out_specs=(vmem,) * 2,
        name="finish",
    )(po, rotation)


def solution(mesh):
    placed = (P("subj", "vert"), P("vert"), P("vert"), P("vert", None))
    return jax.shard_map(
        local,
        mesh=mesh,
        in_specs=placed,
        out_specs=(P("vert", "subj"), P("vert", "subj")),
        check_vma=False,
    )
```
